32 devices in a mesh: blk: 16 (over z, y, x), col: 2 (over core).
Axes of the slice: x: 2, y: 2, z: 4, core: 2. Of those that a mesh axis runs over, the one named last changes fastest.
Arguments:
- embeddings: bfloat16 [6144, 768], P('blk'), may hold values from -1 to 1
- labels: int32 [6144], P('blk'), may hold values from 0 to 999
- landmarks: bfloat16 [512, 768], P(('blk', 'col')), may hold values from -1 to 1
- coeffs: bfloat16 [512, 1000], P(('blk', 'col')), may hold values from -1.25 to 1.25
- widths: bfloat16 [512], P(('blk', 'col')), may hold values from 0.5 to 2
Outputs:
- grad_landmarks: float32 [512, 768], P(('blk', 'col'))
- grad_coeffs: float32 [512, 1000], P(('blk', 'col'))
- grad_embeddings: float32 [6144, 768], P(('blk', 'col'))
The draws below stay inside these ranges and needn't reach their ends.
All inputs are finite; a program needn't handle non-finite values.
Results may differ from the reference program's by a relative error of at most 0.0078.
Values may be sent and summed in bfloat16 or wider, within the bound.
A program may use at most 64 MiB of HBM per device.

```python
import math
import jax
import jax.numpy as jnp
from jax import lax

D = 768
CLASSES = 1000
ROWS = 6144
LANDMARKS = 512
N_BLK = 16


def cluster_centers(key):
    return jax.random.truncated_normal(jax.random.fold_in(key, 101), -4.0, 4.0, (64, D), jnp.float32)


def clustered(key, salt, count):
    centers = cluster_centers(key)
    chosen = jax.random.randint(jax.random.fold_in(key, salt), (count,), 0, 64)
    noise = jax.random.truncated_normal(jax.random.fold_in(key, salt + 1), -4.0, 4.0, (count, D), jnp.float32)
    return (0.9 * centers[chosen] + 0.44 * noise) / math.sqrt(D)


def draw_embeddings(key, part):
    mixed = clustered(key, 202, ROWS)
    return mixed.astype(jnp.bfloat16)


def draw_landmarks(key, part):
    return clustered(key, 303, LANDMARKS).astype(jnp.bfloat16)


def draw_coeffs(key, part):
    values = 0.3 * jax.random.truncated_normal(jax.random.fold_in(key, 403), -4.0, 4.0, (LANDMARKS, CLASSES), jnp.float32)
    return values.astype(jnp.bfloat16)


def place_ends(values, own_key, smallest, largest):
    place = [jax.random.randint(jax.random.fold_in(own_key, axis), (), 0, length) for axis, length in enumerate(values.shape)]
    main_axis = values.shape.index(max(values.shape))
    next_to = place[:main_axis] + [(place[main_axis] + 1) % values.shape[main_axis]] + place[main_axis + 1:]
    return values.at[tuple(place)].set(smallest).at[tuple(next_to)].set(largest)


def levels(rng, shape, cuts, smallest, top_value):
    gain, own = 1.0, jax.random.fold_in(rng, 6)
    for axis_at, blocks in cuts:
        draws = jnp.exp(jax.random.uniform(jax.random.fold_in(own, axis_at), (blocks,), jnp.float32, smallest / len(cuts), top_value / len(cuts)))
        gain = gain * jnp.repeat(draws, shape[axis_at] // blocks).reshape([-1 if axis == axis_at else 1 for axis in range(len(shape))])
    return gain


def setup_inputs(seed: int = 0) -> dict:
    key_list = jax.random.split(jax.random.key(seed), 6)
    embeddings = draw_embeddings(jax.random.fold_in(key_list[5], 71), 0)
    labels = place_ends(jax.random.randint(key_list[1], (ROWS,), 0, CLASSES), jax.random.fold_in(key_list[1], 1), 0, CLASSES - 1).astype(jnp.int32)
    landmarks = draw_landmarks(jax.random.fold_in(key_list[5], 71), 0)
    coeffs = draw_coeffs(jax.random.fold_in(key_list[5], 71), 0)
    widths = jnp.clip(jnp.exp(math.log(2.0) - 1.3862944 * jax.random.uniform(key_list[4], (LANDMARKS,), jnp.float32) ** levels(key_list[4], (LANDMARKS,), ((0, 32),), -0.2, 0.2)), 0.5, 2.0).astype(jnp.bfloat16)
    return dict(embeddings=embeddings, labels=labels, landmarks=landmarks, coeffs=coeffs, widths=widths)


def kernel_block(rows, rows_sq, land, width):
    cross = jnp.dot(rows, land.T, preferred_element_type=jnp.float32)
    land_sq = jnp.sum(jnp.square(land.astype(jnp.float32)), axis=1)
    dist = (rows_sq[:, None] + land_sq[None, :]) - 2.0 * cross
    return jnp.exp(-width.astype(jnp.float32)[None, :] * dist).astype(jnp.bfloat16)


def reference(embeddings, labels, landmarks, coeffs, widths):
    rows_sq = jnp.sum(jnp.square(embeddings.astype(jnp.float32)), axis=1)
    size_b = LANDMARKS // N_BLK
    land_blocks = landmarks.reshape(N_BLK, size_b, D)
    coef_blocks = coeffs.reshape(N_BLK, size_b, CLASSES)
    width_blocks = widths.reshape(N_BLK, size_b)

    def forward(total, item):
        land, coef, width = item
        kern = kernel_block(embeddings, rows_sq, land, width)
        return total + jnp.dot(kern, coef, preferred_element_type=jnp.float32), None

    logits, _ = lax.scan(forward, jnp.zeros((ROWS, CLASSES), jnp.float32), (land_blocks, coef_blocks, width_blocks))
    top = jnp.max(logits, axis=1, keepdims=True)
    expo = jnp.exp(logits - top)
    probs = expo / jnp.sum(expo, axis=1, keepdims=True)
    onehot = (labels[:, None] == jnp.arange(CLASSES, dtype=jnp.int32)[None, :]).astype(jnp.float32)
    grad_logits = (probs - onehot).astype(jnp.bfloat16)

    def backward(carry, item):
        pull_z, pull_rows = carry
        land, coef, width = item
        kern = kernel_block(embeddings, rows_sq, land, width)
        grad_kernel = jnp.dot(grad_logits, coef.T, preferred_element_type=jnp.float32)
        pull = (2.0 * width.astype(jnp.float32)[None, :] * grad_kernel * kern.astype(jnp.float32)).astype(jnp.bfloat16)
        pull_f = pull.astype(jnp.float32)
        grad_coef = jnp.dot(kern.T, grad_logits, preferred_element_type=jnp.float32)
        grad_land = jnp.dot(pull.T, embeddings, preferred_element_type=jnp.float32) - jnp.sum(pull_f, axis=0)[:, None] * land.astype(jnp.float32)
        pull_z = pull_z + jnp.dot(pull, land, preferred_element_type=jnp.float32)
        pull_rows = pull_rows + jnp.sum(pull_f, axis=1)
        return (pull_z, pull_rows), (grad_land, grad_coef)

    start = (jnp.zeros((ROWS, D), jnp.float32), jnp.zeros((ROWS,), jnp.float32))
    (pull_z, pull_rows), (grad_land, grad_coef) = lax.scan(backward, start, (land_blocks, coef_blocks, width_blocks))
    grad_embeddings = pull_z - pull_rows[:, None] * embeddings.astype(jnp.float32)
    return grad_land.reshape(LANDMARKS, D), grad_coef.reshape(LANDMARKS, CLASSES), grad_embeddings
```

```python
import functools

import jax
import jax.numpy as jnp
from jax import lax
from jax.experimental import pallas as pl
from jax.experimental.pallas import tpu as pltpu
from jax.sharding import PartitionSpec as P


def from_behind(block, axis, distance):
    devices = range(lax.axis_size(axis))
    route = [((i - distance) % len(devices), i) for i in devices]
    return lax.ppermute(block, axis, route)


def block_kernel(rows, rows_sq, land, width):
    cross = lax.dot_general(
        land, rows, (((1,), (1,)), ((), ())), preferred_element_type=jnp.float32
    )
    land_sq = jnp.sum(jnp.square(land.astype(jnp.float32)), axis=1)
    dist = rows_sq[None, :] + land_sq[:, None] - 2.0 * cross
    return jnp.exp(-width.astype(jnp.float32)[:, None] * dist).astype(jnp.bfloat16)


def class_logits(kern_t, coef):
    return lax.dot_general(
        kern_t, coef, (((0,), (0,)), ((), ())), preferred_element_type=jnp.float32
    )


def logit_gradient(logits, labels):
    top = jnp.max(logits, axis=1, keepdims=True)
    expo = jnp.exp(logits - top)
    probs = expo / jnp.sum(expo, axis=1, keepdims=True)
    classes = lax.broadcasted_iota(jnp.int32, logits.shape, 1)
    onehot = (classes == labels[:, None]).astype(jnp.float32)
    return (probs - onehot).astype(jnp.bfloat16)


def grad_terms(land, coef, width, kern_t, rows, grad_rows):
    grad_kernel = lax.dot_general(
        coef, grad_rows, (((1,), (1,)), ((), ())), preferred_element_type=jnp.float32
    )
    pull = (
        2.0 * width.astype(jnp.float32)[:, None] * grad_kernel * kern_t.astype(jnp.float32)
    ).astype(jnp.bfloat16)
    grad_coef = jnp.dot(kern_t, grad_rows, preferred_element_type=jnp.float32)
    grad_land = jnp.dot(pull, rows, preferred_element_type=jnp.float32) - jnp.sum(
        pull.astype(jnp.float32), axis=1
    )[:, None] * land.astype(jnp.float32)
    return (grad_land, grad_coef, pull)


def project_rows(pull, land):
    return lax.dot_general(pull, land, (((0,), (0,)), ((), ())), preferred_element_type=jnp.float32)


def target_block(position, step, blocks):
    return (position - step - 1) % blocks


def local(embeddings, labels, landmarks, coeffs, widths):
    rows_sq = jnp.sum(jnp.square(embeddings.astype(jnp.float32)), axis=1)
    width_d = embeddings.shape[1]
    classes = coeffs.shape[1]
    size_b = landmarks.shape[0]
    blocks = lax.axis_size("blk")
    position = lax.axis_index("blk")
    all_land, all_coef, all_width = (
        lax.all_gather(landmarks, "blk", axis=0, tiled=True),
        lax.all_gather(coeffs, "blk", axis=0, tiled=True),
        lax.all_gather(widths, "blk", axis=0, tiled=True),
    )
    kern_all = block_kernel(embeddings, rows_sq, all_land, all_width)
    partial_value = class_logits(kern_all, all_coef)
    logits = lax.psum(partial_value, "col")
    grad_rows = logit_gradient(logits, labels)
    sections = ((True, 0, size_b),)

    def pass_on(values):
        return from_behind((values[0], values[1]), "blk", 1)

    empty = tuple(
        (
            (jnp.zeros((size, width_d), jnp.float32), jnp.zeros((size, classes), jnp.float32))
            for upward, low, size in sections
        )
    )
    land_all, coef_all, pull_all = grad_terms(
        all_land, all_coef, all_width, kern_all, embeddings, grad_rows
    )
    pull_z = project_rows(pull_all, all_land)
    pull_rows = jnp.sum(pull_all.astype(jnp.float32), axis=0)

    def select(values, block, low, size):
        return lax.dynamic_slice_in_dim(values, block * size_b + low, size, 0)

    def cached_step(step, accums):
        moved = []
        for index, (upward, low, size) in enumerate(sections):
            block = target_block(position, step, blocks)
            total = (
                accums[index][0] + select(land_all, block, low, size),
                accums[index][1] + select(coef_all, block, low, size),
            )
            moved.append(pass_on(total))
        return tuple(moved)

    accums = lax.fori_loop(0, blocks - 1, cached_step, empty)
    finals = [
        (
            accums[index][0] + select(land_all, position, low, size),
            accums[index][1] + select(coef_all, position, low, size),
        )
        for index, (upward, low, size) in enumerate(sections)
    ]
    grad_landmarks = jnp.concatenate([item[0] for item in finals], axis=0)
    grad_coeffs = jnp.concatenate([item[1] for item in finals], axis=0)
    local_rows = pull_z - pull_rows[:, None] * embeddings.astype(jnp.float32)
    grad_embeddings = lax.psum_scatter(local_rows, "col", scatter_dimension=0, tiled=True)
    return (grad_landmarks, grad_coeffs, grad_embeddings)


NT = (((1,), (1,)), ((), ()))
TN = (((0,), (0,)), ((), ()))


def fused_kernel(
    classes, emb_ref, lab_ref, land_ref, coef_ref, width_ref,
    out_land, out_coef, out_emb,
    table, emb, kern, pull, logits, grad, acc, emb_out,
    to_core, from_core, to_second, from_second, to_first, from_first, to_z, from_z,
    send_sem, z_sem, first_sem, second_sem, core_sem, back_sem, local_sem,
):
    blk, col = lax.axis_index("blk"), lax.axis_index("col")
    size, depth = land_ref.shape
    wide = table.shape[1]
    rows = emb.shape[0]
    slab, half = 4 * size, 8 * size
    other = 1 - col
    x, y, z = blk % 2, (blk // 2) % 2, blk // 4
    my1 = x * other + y * col
    my2 = y * other + x * col
    first = (blk + (1 - 2 * my1) * (1 + col), col)
    second = (blk + (1 - 2 * my2) * (2 - col), col)
    core = (blk, other)
    along_z = [(((z + k) % 4) * 4 + blk % 4, col) for k in range(4)]

    def base(c, p2, p1):
        return ((c * 2 + p2) * 2 + p1) * slab

    def piece(start, k):
        return pl.ds(pl.multiple_of(start + ((z - k + 4) % 4) * size, size), size)

    load = pltpu.make_async_copy(
        emb_ref.at[pl.ds(pl.multiple_of(col * rows, 64), rows)], emb, local_sem.at[0]
    )
    load.start()

    barrier = pltpu.get_barrier_semaphore()
    peers = [first, second, core] + along_z[1:]
    for peer in peers:
        pl.semaphore_signal(barrier, inc=1, device_id=peer, device_id_type=pl.DeviceIdType.MESH)

    own = piece(base(col, my2, my1), 0)
    eye = lax.broadcasted_iota(jnp.int32, (size, size), 0) == lax.broadcasted_iota(
        jnp.int32, (size, size), 1
    )
    width_col = jnp.sum(
        jnp.where(eye, width_ref[...].astype(jnp.float32), 0.0), axis=1, keepdims=True
    )
    tail = wide - 128
    split = tail - depth
    lanes = lax.broadcasted_iota(jnp.int32, (size, 128), 1)
    last = jnp.concatenate(
        [
            coef_ref[:, split:].astype(jnp.float32),
            jnp.zeros((size, 128 - (classes - split)), jnp.float32),
        ],
        axis=1,
    )
    last = jnp.where(lanes == classes - split, width_col, last)
    table[own, :depth] = land_ref[...]
    table[own, depth:tail] = coef_ref[:, :split]
    table[own, tail:] = last.astype(jnp.bfloat16)

    pl.semaphore_wait(barrier, len(peers))

    sends = []

    def send(src, dst, recv, device):
        copy = pltpu.make_async_remote_copy(
            src_ref=src, dst_ref=dst, send_sem=send_sem.at[len(sends)], recv_sem=recv,
            device_id=device, device_id_type=pl.DeviceIdType.MESH,
        )
        copy.start()
        sends.append(copy)

    def arrived(dst, recv):
        pltpu.make_async_remote_copy(
            src_ref=dst, dst_ref=dst, send_sem=send_sem.at[0], recv_sem=recv,
            device_id=core, device_id_type=pl.DeviceIdType.MESH,
        ).wait_recv()

    def put(where, recv, device):
        send(table.at[where], table.at[where], recv, device)

    slab_a = base(col, my2, my1)
    slab_b = base(col, my2, 1 - my1)
    slab_c = base(col, 1 - my2, my1)
    slab_d = base(col, 1 - my2, 1 - my1)
    for k in (1, 3, 2):
        put(own, z_sem.at[k], along_z[k])
    put(own, first_sem.at[0], first)
    put(own, second_sem.at[0], second)
    put(own, core_sem.at[0], core)

    load.wait()
    emb_f = emb[...].astype(jnp.float32)
    eye_rows = lax.broadcasted_iota(jnp.int32, (rows, rows), 0) == lax.broadcasted_iota(
        jnp.int32, (rows, rows), 1
    )
    rows_sq = jnp.sum(jnp.square(emb_f), axis=1, keepdims=True)
    rows_sq = jnp.sum(jnp.where(eye_rows, rows_sq, 0.0), axis=0, keepdims=True)

    for k in (1, 3, 2):
        where = piece(slab_a, k)
        arrived(table.at[where], z_sem.at[k])
        put(where, first_sem.at[k], first)
        put(where, second_sem.at[k], second)
        put(where, core_sem.at[k], core)

    def widths_of(where):
        end = table[where, tail:].astype(jnp.float32)
        at = lax.broadcasted_iota(jnp.int32, end.shape, 1) == classes - split
        return jnp.sum(jnp.where(at, end, 0.0), axis=1, keepdims=True)

    def forward(start, fresh):
        where = pl.ds(pl.multiple_of(start, half), half)
        land = table[where, :depth]
        cross = lax.dot_general(land, emb[...], NT, preferred_element_type=jnp.float32)
        land_sq = jnp.sum(jnp.square(land.astype(jnp.float32)), axis=1, keepdims=True)
        dist = (rows_sq + land_sq) - 2.0 * cross
        value = jnp.exp(-widths_of(where) * dist).astype(jnp.bfloat16)
        kern[where, :] = value
        part = lax.dot_general(
            value, table[where, depth:], TN, preferred_element_type=jnp.float32
        )
        if fresh:
            logits[...] = part
        else:
            logits[...] += part

    for k in (0, 1, 3, 2):
        where = piece(slab_b, k)
        arrived(table.at[where], first_sem.at[k])
        put(where, second_sem.at[4 + k], second)
        put(where, core_sem.at[4 + k], core)
    forward(base(col, my2, 0), True)
    for n, start in enumerate((base(other, my1, my2), base(other, my1, 1 - my2))):
        for k in range(4):
            arrived(table.at[piece(start, k)], core_sem.at[4 * n + k])
    forward(base(other, my1, 0), False)
    for n, start in enumerate((slab_c, slab_d)):
        for k in (0, 1, 3, 2):
            where = piece(start, k)
            arrived(table.at[where], second_sem.at[4 * n + k])
            put(where, core_sem.at[8 + 4 * n + k], core)
    forward(base(col, 1 - my2, 0), False)
    for n, start in enumerate((base(other, 1 - my1, my2), base(other, 1 - my1, 1 - my2))):
        for k in range(4):
            arrived(table.at[piece(start, k)], core_sem.at[8 + 4 * n + k])
    forward(base(other, 1 - my1, 0), False)

    all_rows = lab_ref.shape[1]
    mine = lax.broadcasted_iota(jnp.int32, (rows, all_rows), 1) == (
        lax.broadcasted_iota(jnp.int32, (rows, all_rows), 0) + col * rows
    )
    label = jnp.sum(
        jnp.where(mine, lab_ref[...].astype(jnp.float32), 0.0), axis=1, keepdims=True
    ).astype(jnp.int32)
    place = lax.broadcasted_iota(jnp.int32, logits.shape, 1)
    value = jnp.where(place < classes, logits[...], -jnp.inf)
    expo = jnp.exp(value - jnp.max(value, axis=1, keepdims=True))
    probs = expo / jnp.sum(expo, axis=1, keepdims=True)
    grad[...] = (probs - jnp.where(place == label, 1.0, 0.0)).astype(jnp.bfloat16)

    grad_kernel = lax.dot_general(
        table[:, depth:], grad[...], NT, preferred_element_type=jnp.float32
    )
    pull[...] = (
        2.0 * widths_of(slice(None)) * grad_kernel * kern[...].astype(jnp.float32)
    ).astype(jnp.bfloat16)

    def terms(start):
        where = pl.ds(pl.multiple_of(start, half), half)
        tug = pull[where, :]
        land = jnp.dot(tug, emb[...], preferred_element_type=jnp.float32)
        land -= jnp.sum(tug.astype(jnp.float32), axis=1, keepdims=True) * table[
            where, :depth
        ].astype(jnp.float32)
        coef = jnp.dot(kern[where, :], grad[...], preferred_element_type=jnp.float32)
        return land, coef

    def part(index):
        return pl.ds(pl.multiple_of(index * slab, slab), slab)

    def for_core(n, p2):
        land, coef = terms(base(other, p2, 0))
        to_core[n, :, :depth] = land.astype(jnp.bfloat16)
        to_core[n, :, depth:] = coef.astype(jnp.bfloat16)
        for m, p1 in enumerate((1 - my2, my2)):
            send(
                to_core.at[n, part(p1)], from_core.at[n, part(p1)],
                back_sem.at[2 * n + m], core,
            )

    def for_self(n, p2):
        land, coef = terms(base(col, p2, 0))
        acc[n, :, :depth] = land
        acc[n, :, depth:] = coef

    for_core(0, 1 - my1)
    for_self(0, 1 - my2)
    for m, p1 in enumerate((1 - my1, my1)):
        arrived(from_core.at[0, part(p1)], back_sem.at[m])
        total = acc[0, part(p1), :] + from_core[0, part(p1), :].astype(jnp.float32)
        to_second[m] = total.astype(jnp.bfloat16)
        send(to_second.at[m], from_second.at[m], back_sem.at[4 + m], second)
    for_core(1, my1)
    for_self(1, my2)

    tug = pull[...].T
    drawn = jnp.dot(tug, table[:, :depth], preferred_element_type=jnp.float32)
    emb_out[...] = drawn - jnp.sum(
        tug.astype(jnp.float32), axis=1, keepdims=True
    ) * emb[...].astype(jnp.float32)
    store = pltpu.make_async_copy(emb_out, out_emb, local_sem.at[1])
    store.start()

    arrived(from_core.at[1, part(1 - my1)], back_sem.at[2])
    arrived(from_second.at[0], back_sem.at[4])
    total = (
        acc[1, part(1 - my1), :]
        + from_core[1, part(1 - my1), :].astype(jnp.float32)
        + from_second[0].astype(jnp.float32)
    )
    to_first[...] = total.astype(jnp.bfloat16)
    send(to_first, from_first, back_sem.at[6], first)
    arrived(from_core.at[1, part(my1)], back_sem.at[3])
    arrived(from_second.at[1], back_sem.at[5])
    total = (
        acc[1, part(my1), :]
        + from_core[1, part(my1), :].astype(jnp.float32)
        + from_second[1].astype(jnp.float32)
    )
    arrived(from_first, back_sem.at[6])
    total += from_first[...].astype(jnp.float32)
    acc[0, :slab, :] = total
    to_z[...] = total.astype(jnp.bfloat16)
    for k in (2, 1, 3):
        target = pl.ds(pl.multiple_of(((z + k) % 4) * size, size), size)
        send(to_z.at[target], from_z.at[k - 1], back_sem.at[6 + k], along_z[k])
    result = acc[0, pl.ds(pl.multiple_of(z * size, size), size), :]
    for k in (1, 3, 2):
        arrived(from_z.at[k - 1], back_sem.at[6 + k])
        result += from_z[k - 1].astype(jnp.float32)
    out_land[...] = result[:, :depth]
    out_coef[...] = result[:, depth : depth + classes]

    store.wait()
    for copy in sends:
        copy.wait_send()


def fused(embeddings, labels, landmarks, coeffs, widths):
    size, depth = landmarks.shape
    classes = coeffs.shape[1]
    rows = embeddings.shape[0] // 2
    padded = (classes // 128 + 1) * 128
    wide = depth + padded
    count, slab, half = 32 * size, 4 * size, 8 * size
    vmem = pl.BlockSpec(memory_space=pltpu.VMEM)
    anywhere = pl.BlockSpec(memory_space=pl.ANY)
    bf16, f32 = jnp.bfloat16, jnp.float32
    return pl.pallas_call(
        functools.partial(fused_kernel, classes),
        out_shape=(
            jax.ShapeDtypeStruct((size, depth), f32),
            jax.ShapeDtypeStruct((size, classes), f32),
            jax.ShapeDtypeStruct((rows, depth), f32),
        ),
        in_specs=[anywhere, vmem, vmem, vmem, vmem],
        out_specs=(vmem, vmem, anywhere),
        scratch_shapes=[
            pltpu.VMEM((count, wide), bf16),
            pltpu.VMEM((rows, depth), bf16),
            pltpu.VMEM((count, rows), bf16),
            pltpu.VMEM((count, rows), bf16),
            pltpu.VMEM((rows, padded), f32),
            pltpu.VMEM((rows, padded), bf16),
            pltpu.VMEM((2, half, wide), f32),
            pltpu.VMEM((rows, depth), f32),
            pltpu.VMEM((2, half, wide), bf16),
            pltpu.VMEM((2, half, wide), bf16),
            pltpu.VMEM((2, slab, wide), bf16),
            pltpu.VMEM((2, slab, wide), bf16),
            pltpu.VMEM((slab, wide), bf16),
            pltpu.VMEM((slab, wide), bf16),
            pltpu.VMEM((slab, wide), bf16),
            pltpu.VMEM((3, size, wide), bf16),
            pltpu.SemaphoreType.DMA((48,)),
            pltpu.SemaphoreType.DMA((4,)),
            pltpu.SemaphoreType.DMA((4,)),
            pltpu.SemaphoreType.DMA((8,)),
            pltpu.SemaphoreType.DMA((16,)),
            pltpu.SemaphoreType.DMA((10,)),
            pltpu.SemaphoreType.DMA((2,)),
        ],
        compiler_params=pltpu.CompilerParams(
            collective_id=0, has_side_effects=True, vmem_limit_bytes=48 * 2**20
        ),
    )(embeddings, labels[None, :], landmarks, coeffs, widths[None, :])


def fits_fused(mesh):
    return mesh.shape["blk"] == 16 and mesh.shape["col"] == 2


def solution(mesh):
    return jax.shard_map(
        fused if fits_fused(mesh) else local,
        mesh=mesh,
        in_specs=(
            P("blk", None),
            P("blk"),
            P(("blk", "col"), None),
            P(("blk", "col"), None),
            P(("blk", "col")),
        ),
        out_specs=(P(("blk", "col"), None), P(("blk", "col"), None), P(("blk", "col"), None)),
        check_vma=False,
    )
```

```python
import functools

import jax
import jax.numpy as jnp
from jax import lax
from jax.experimental import pallas as pl
from jax.experimental.pallas import tpu as pltpu
from jax.sharding import PartitionSpec as P


def from_behind(block, axis, distance):
    devices = range(lax.axis_size(axis))
    route = [((i - distance) % len(devices), i) for i in devices]
    return lax.ppermute(block, axis, route)


def block_kernel(rows, rows_sq, land, width):
    cross = lax.dot_general(
        land, rows, (((1,), (1,)), ((), ())), preferred_element_type=jnp.float32
    )
    land_sq = jnp.sum(jnp.square(land.astype(jnp.float32)), axis=1)
    dist = rows_sq[None, :] + land_sq[:, None] - 2.0 * cross
    return jnp.exp(-width.astype(jnp.float32)[:, None] * dist).astype(jnp.bfloat16)


def class_logits(kern_t, coef):
    return lax.dot_general(
        kern_t, coef, (((0,), (0,)), ((), ())), preferred_element_type=jnp.float32
    )


def logit_gradient(logits, labels):
    top = jnp.max(logits, axis=1, keepdims=True)
    expo = jnp.exp(logits - top)
    probs = expo / jnp.sum(expo, axis=1, keepdims=True)
    classes = lax.broadcasted_iota(jnp.int32, logits.shape, 1)
    onehot = (classes == labels[:, None]).astype(jnp.float32)
    return (probs - onehot).astype(jnp.bfloat16)


def grad_terms(land, coef, width, kern_t, rows, grad_rows):
    grad_kernel = lax.dot_general(
        coef, grad_rows, (((1,), (1,)), ((), ())), preferred_element_type=jnp.float32
    )
    pull = (
        2.0 * width.astype(jnp.float32)[:, None] * grad_kernel * kern_t.astype(jnp.float32)
    ).astype(jnp.bfloat16)
    grad_coef = jnp.dot(kern_t, grad_rows, preferred_element_type=jnp.float32)
    grad_land = jnp.dot(pull, rows, preferred_element_type=jnp.float32) - jnp.sum(
        pull.astype(jnp.float32), axis=1
    )[:, None] * land.astype(jnp.float32)
    return (grad_land, grad_coef, pull)


def project_rows(pull, land):
    return lax.dot_general(pull, land, (((0,), (0,)), ((), ())), preferred_element_type=jnp.float32)


def target_block(position, step, blocks):
    return (position - step - 1) % blocks


def local(embeddings, labels, landmarks, coeffs, widths):
    rows_sq = jnp.sum(jnp.square(embeddings.astype(jnp.float32)), axis=1)
    width_d = embeddings.shape[1]
    classes = coeffs.shape[1]
    size_b = landmarks.shape[0]
    blocks = lax.axis_size("blk")
    position = lax.axis_index("blk")
    all_land, all_coef, all_width = (
        lax.all_gather(landmarks, "blk", axis=0, tiled=True),
        lax.all_gather(coeffs, "blk", axis=0, tiled=True),
        lax.all_gather(widths, "blk", axis=0, tiled=True),
    )
    kern_all = block_kernel(embeddings, rows_sq, all_land, all_width)
    partial_value = class_logits(kern_all, all_coef)
    logits = lax.psum(partial_value, "col")
    grad_rows = logit_gradient(logits, labels)
    sections = ((True, 0, size_b),)

    def pass_on(values):
        return from_behind((values[0], values[1]), "blk", 1)

    empty = tuple(
        (
            (jnp.zeros((size, width_d), jnp.float32), jnp.zeros((size, classes), jnp.float32))
            for upward, low, size in sections
        )
    )
    land_all, coef_all, pull_all = grad_terms(
        all_land, all_coef, all_width, kern_all, embeddings, grad_rows
    )
    pull_z = project_rows(pull_all, all_land)
    pull_rows = jnp.sum(pull_all.astype(jnp.float32), axis=0)

    def select(values, block, low, size):
        return lax.dynamic_slice_in_dim(values, block * size_b + low, size, 0)

    def cached_step(step, accums):
        moved = []
        for index, (upward, low, size) in enumerate(sections):
            block = target_block(position, step, blocks)
            total = (
                accums[index][0] + select(land_all, block, low, size),
                accums[index][1] + select(coef_all, block, low, size),
            )
            moved.append(pass_on(total))
        return tuple(moved)

    accums = lax.fori_loop(0, blocks - 1, cached_step, empty)
    finals = [
        (
            accums[index][0] + select(land_all, position, low, size),
            accums[index][1] + select(coef_all, position, low, size),
        )
        for index, (upward, low, size) in enumerate(sections)
    ]
    grad_landmarks = jnp.concatenate([item[0] for item in finals], axis=0)
    grad_coeffs = jnp.concatenate([item[1] for item in finals], axis=0)
    local_rows = pull_z - pull_rows[:, None] * embeddings.astype(jnp.float32)
    grad_embeddings = lax.psum_scatter(local_rows, "col", scatter_dimension=0, tiled=True)
    return (grad_landmarks, grad_coeffs, grad_embeddings)


NT = (((1,), (1,)), ((), ()))
TN = (((0,), (0,)), ((), ()))


def fused_kernel(
    classes, emb_hbm, lab_hbm, land_hbm, coef_hbm, width_hbm,
    out_land, out_coef, out_emb,
    emb, lab_ref, land_ref, coef_ref, width_ref,
    table, kern, pull, pull_t, logits, grad, acc, emb_out,
    to_core, from_core, to_second, from_second, to_first, from_first, to_z, from_z,
    send_sem, z_sem, first_sem, second_sem, core_sem, back_sem, piece_sem, local_sem,
):
    blk, col = lax.axis_index("blk"), lax.axis_index("col")
    size, depth = land_ref.shape
    wide = table.shape[1]
    rows = emb.shape[0]
    slab, half = 4 * size, 8 * size
    other = 1 - col
    x, y, z = blk % 2, (blk // 2) % 2, blk // 4
    my1 = x * other + y * col
    my2 = y * other + x * col
    first = (blk + (1 - 2 * my1) * (1 + col), col)
    second = (blk + (1 - 2 * my2) * (2 - col), col)
    core = (blk, other)
    along_z = [(((z + k) % 4) * 4 + blk % 4, col) for k in range(4)]

    def base(c, p2, p1):
        return ((c * 2 + p2) * 2 + p1) * slab

    def piece(start, k):
        return pl.ds(pl.multiple_of(start + ((z - k + 4) % 4) * size, size), size)

    mine = emb_hbm.at[pl.ds(pl.multiple_of(col * rows, 64), rows)]
    loads = [
        pltpu.make_async_copy(src, dst, local_sem.at[n])
        for n, (src, dst) in enumerate((
            (land_hbm, land_ref), (coef_hbm, coef_ref), (width_hbm, width_ref),
            (lab_hbm, lab_ref), (mine, emb),
        ))
    ]
    for load in loads:
        load.start()

    barrier = pltpu.get_barrier_semaphore()
    peers = [first, second, core] + along_z[1:]
    for peer in peers:
        pl.semaphore_signal(barrier, inc=1, device_id=peer, device_id_type=pl.DeviceIdType.MESH)

    own = piece(base(col, my2, my1), 0)
    for load in loads[:3]:
        load.wait()
    eye = lax.broadcasted_iota(jnp.int32, (size, size), 0) == lax.broadcasted_iota(
        jnp.int32, (size, size), 1
    )
    width_col = jnp.sum(
        jnp.where(eye, width_ref[...].astype(jnp.float32), 0.0), axis=1, keepdims=True
    )
    tail = wide - 128
    split = tail - depth
    lanes = lax.broadcasted_iota(jnp.int32, (size, 128), 1)
    last = jnp.concatenate(
        [
            coef_ref[:, split:].astype(jnp.float32),
            jnp.zeros((size, 128 - (classes - split)), jnp.float32),
        ],
        axis=1,
    )
    last = jnp.where(lanes == classes - split, width_col, last)
    table[own, :depth] = land_ref[...]
    table[own, depth:tail] = coef_ref[:, :split]
    table[own, tail:] = last.astype(jnp.bfloat16)

    pl.semaphore_wait(barrier, len(peers))

    sends = []

    def send(src, dst, recv, device):
        copy = pltpu.make_async_remote_copy(
            src_ref=src, dst_ref=dst, send_sem=send_sem.at[len(sends)], recv_sem=recv,
            device_id=device, device_id_type=pl.DeviceIdType.MESH,
        )
        copy.start()
        sends.append(copy)

    def arrived(dst, recv):
        pltpu.make_async_remote_copy(
            src_ref=dst, dst_ref=dst, send_sem=send_sem.at[0], recv_sem=recv,
            device_id=core, device_id_type=pl.DeviceIdType.MESH,
        ).wait_recv()

    def put(where, recv, device):
        send(table.at[where], table.at[where], recv, device)

    slab_a = base(col, my2, my1)
    slab_b = base(col, my2, 1 - my1)
    slab_c = base(col, 1 - my2, my1)
    slab_d = base(col, 1 - my2, 1 - my1)
    for k in (1, 3, 2):
        put(own, z_sem.at[k], along_z[k])
    put(own, first_sem.at[0], first)
    put(own, second_sem.at[0], second)
    put(own, core_sem.at[0], core)

    for load in loads[3:]:
        load.wait()
    emb_f = emb[...].astype(jnp.float32)
    eye_rows = lax.broadcasted_iota(jnp.int32, (rows, rows), 0) == lax.broadcasted_iota(
        jnp.int32, (rows, rows), 1
    )
    rows_sq = jnp.sum(jnp.square(emb_f), axis=1, keepdims=True)
    rows_sq = jnp.sum(jnp.where(eye_rows, rows_sq, 0.0), axis=0, keepdims=True)

    for k in (1, 3, 2):
        where = piece(slab_a, k)
        arrived(table.at[where], z_sem.at[k])
        put(where, first_sem.at[k], first)
        put(where, second_sem.at[k], second)
        put(where, core_sem.at[k], core)

    def widths_of(where):
        end = table[where, tail:].astype(jnp.float32)
        at = lax.broadcasted_iota(jnp.int32, end.shape, 1) == classes - split
        return jnp.sum(jnp.where(at, end, 0.0), axis=1, keepdims=True)

    def forward(start, fresh):
        where = pl.ds(pl.multiple_of(start, half), half)
        land = table[where, :depth]
        cross = lax.dot_general(land, emb[...], NT, preferred_element_type=jnp.float32)
        land_sq = jnp.sum(jnp.square(land.astype(jnp.float32)), axis=1, keepdims=True)
        dist = (rows_sq + land_sq) - 2.0 * cross
        value = jnp.exp(-widths_of(where) * dist).astype(jnp.bfloat16)
        kern[where, :] = value
        part = lax.dot_general(
            value, table[where, depth:], TN, preferred_element_type=jnp.float32
        )
        if fresh:
            logits[...] = part
        else:
            logits[...] += part

    for k in (0, 1, 3, 2):
        where = piece(slab_b, k)
        arrived(table.at[where], first_sem.at[k])
        put(where, second_sem.at[4 + k], second)
        put(where, core_sem.at[4 + k], core)
    forward(base(col, my2, 0), True)
    for n, start in enumerate((base(other, my1, my2), base(other, my1, 1 - my2))):
        for k in range(4):
            arrived(table.at[piece(start, k)], core_sem.at[4 * n + k])
    forward(base(other, my1, 0), False)
    for n, start in enumerate((slab_c, slab_d)):
        for k in (0, 1, 3, 2):
            where = piece(start, k)
            arrived(table.at[where], second_sem.at[4 * n + k])
            put(where, core_sem.at[8 + 4 * n + k], core)
    forward(base(col, 1 - my2, 0), False)
    for n, start in enumerate((base(other, 1 - my1, my2), base(other, 1 - my1, 1 - my2))):
        for k in range(4):
            arrived(table.at[piece(start, k)], core_sem.at[8 + 4 * n + k])
    forward(base(other, 1 - my1, 0), False)

    all_rows = lab_ref.shape[0]
    mine = lax.broadcasted_iota(jnp.int32, (rows, all_rows), 1) == (
        lax.broadcasted_iota(jnp.int32, (rows, all_rows), 0) + col * rows
    )
    label = jnp.sum(
        jnp.where(mine, lab_ref[...].astype(jnp.float32)[None, :], 0.0), axis=1, keepdims=True
    ).astype(jnp.int32)
    place = lax.broadcasted_iota(jnp.int32, logits.shape, 1)
    value = jnp.where(place < classes, logits[...], -jnp.inf)
    expo = jnp.exp(value - jnp.max(value, axis=1, keepdims=True))
    probs = expo / jnp.sum(expo, axis=1, keepdims=True)
    grad[...] = (probs - jnp.where(place == label, 1.0, 0.0)).astype(jnp.bfloat16)

    def terms(start):
        where = pl.ds(pl.multiple_of(start, half), half)
        grad_kernel = lax.dot_general(
            table[where, depth:], grad[...], NT, preferred_element_type=jnp.float32
        )
        tug = (
            2.0 * widths_of(where) * grad_kernel * kern[where, :].astype(jnp.float32)
        ).astype(jnp.bfloat16)
        pull[where, :] = tug
        land = jnp.dot(tug, emb[...], preferred_element_type=jnp.float32)
        land -= jnp.sum(tug.astype(jnp.float32), axis=1, keepdims=True) * table[
            where, :depth
        ].astype(jnp.float32)
        coef = jnp.dot(kern[where, :], grad[...], preferred_element_type=jnp.float32)
        return land, coef

    def part(index):
        return pl.ds(pl.multiple_of(index * slab, slab), slab)

    def for_core(n, p2):
        land, coef = terms(base(other, p2, 0))
        to_core[n, :, :depth] = land.astype(jnp.bfloat16)
        to_core[n, :, depth:] = coef.astype(jnp.bfloat16)
        for m, p1 in enumerate((1 - my2, my2)):
            send(
                to_core.at[n, part(p1)], from_core.at[n, part(p1)],
                back_sem.at[2 * n + m], core,
            )

    def for_self(n, p2):
        land, coef = terms(base(col, p2, 0))
        acc[n, :, :depth] = land
        acc[n, :, depth:] = coef

    def target(p1, k):
        start = p1 * slab + ((z + k) % 4) * size
        return pl.ds(pl.multiple_of(start, size), size)

    order = (2, 1, 3, 0)
    for_core(0, 1 - my1)
    for_self(0, 1 - my2)
    for m, p1 in enumerate((1 - my1, my1)):
        arrived(from_core.at[0, part(p1)], back_sem.at[m])
    for n, k in enumerate(order):
        for m, p1 in enumerate((1 - my1, my1)):
            where = target(p1, k)
            total = acc[0, where, :] + from_core[0, where, :].astype(jnp.float32)
            to_second[n, m] = total.astype(jnp.bfloat16)
            send(to_second.at[n, m], from_second.at[n, m], piece_sem.at[n, m], second)
    for_core(1, my1)
    for_self(1, my2)
    for m, p1 in enumerate((1 - my1, my1)):
        arrived(from_core.at[1, part(p1)], back_sem.at[2 + m])

    def summed(n, m, p1, k):
        where = target(p1, k)
        arrived(from_second.at[n, m], piece_sem.at[n, m])
        return (
            acc[1, where, :]
            + from_core[1, where, :].astype(jnp.float32)
            + from_second[n, m].astype(jnp.float32)
        )

    def pass_first(n):
        to_first[n] = summed(n, 0, 1 - my1, order[n]).astype(jnp.bfloat16)
        send(to_first.at[n], from_first.at[n], piece_sem.at[n, 2], first)

    def collect(n):
        total = summed(n, 1, my1, order[n])
        arrived(from_first.at[n], piece_sem.at[n, 2])
        return total + from_first[n].astype(jnp.float32)

    def pass_z(n):
        to_z[n] = collect(n).astype(jnp.bfloat16)
        send(to_z.at[n], from_z.at[n], piece_sem.at[n, 3], along_z[order[n]])

    def project(n):
        where = pl.ds(n * slab, slab)
        tug = pull_t[where, :]
        drawn = jnp.dot(tug, table[:, :depth], preferred_element_type=jnp.float32)
        emb_out[where, :] = drawn - jnp.sum(
            tug.astype(jnp.float32), axis=1, keepdims=True
        ) * emb[where, :].astype(jnp.float32)

    pull_t[...] = pull[...].T
    pass_first(0)
    project(0)
    pass_first(1)
    pass_z(0)
    project(1)
    pass_first(2)
    pass_z(1)
    project(2)
    store = pltpu.make_async_copy(emb_out, out_emb, local_sem.at[5])
    store.start()
    pass_first(3)
    pass_z(2)
    result = collect(3)
    for n in (1, 2, 0):
        arrived(from_z.at[n], piece_sem.at[n, 3])
        result += from_z[n].astype(jnp.float32)
    out_land[...] = result[:, :depth]
    out_coef[...] = result[:, depth : depth + classes]

    store.wait()
    for copy in sends:
        copy.wait_send()


def place_kernel(land, coef, emb, out_land, out_coef, out_emb, sem):
    copies = [
        pltpu.make_async_copy(src, dst, sem.at[n])
        for n, (src, dst) in enumerate(((emb, out_emb), (coef, out_coef), (land, out_land)))
    ]
    for copy in copies:
        copy.start()
    for copy in copies:
        copy.wait()


def fused(embeddings, labels, landmarks, coeffs, widths):
    size, depth = landmarks.shape
    classes = coeffs.shape[1]
    rows = embeddings.shape[0] // 2
    padded = (classes // 128 + 1) * 128
    wide = depth + padded
    count, half = 32 * size, 8 * size
    vmem = pl.BlockSpec(memory_space=pltpu.VMEM)
    hbm = pl.BlockSpec(memory_space=pltpu.HBM)
    anywhere = pl.BlockSpec(memory_space=pl.ANY)
    bf16, f32 = jnp.bfloat16, jnp.float32
    out_shape = (
        jax.ShapeDtypeStruct((size, depth), f32),
        jax.ShapeDtypeStruct((size, classes), f32),
        jax.ShapeDtypeStruct((rows, depth), f32),
    )
    results = pl.pallas_call(
        functools.partial(fused_kernel, classes),
        out_shape=out_shape,
        in_specs=[hbm] * 5,
        out_specs=(vmem, vmem, anywhere),
        scratch_shapes=[
            pltpu.VMEM((rows, depth), bf16),
            pltpu.VMEM(labels.shape, labels.dtype),
            pltpu.VMEM(landmarks.shape, bf16),
            pltpu.VMEM(coeffs.shape, bf16),
            pltpu.VMEM((1, size), bf16),
            pltpu.VMEM((count, wide), bf16),
            pltpu.VMEM((count, rows), bf16),
            pltpu.VMEM((count, rows), bf16),
            pltpu.VMEM((rows, count), bf16),
            pltpu.VMEM((rows, padded), f32),
            pltpu.VMEM((rows, padded), bf16),
            pltpu.VMEM((2, half, wide), f32),
            pltpu.VMEM((rows, depth), f32),
            pltpu.VMEM((2, half, wide), bf16),
            pltpu.VMEM((2, half, wide), bf16),
            pltpu.VMEM((4, 2, size, wide), bf16),
            pltpu.VMEM((4, 2, size, wide), bf16),
            pltpu.VMEM((4, size, wide), bf16),
            pltpu.VMEM((4, size, wide), bf16),
            pltpu.VMEM((3, size, wide), bf16),
            pltpu.VMEM((3, size, wide), bf16),
            pltpu.SemaphoreType.DMA((50,)),
            pltpu.SemaphoreType.DMA((4,)),
            pltpu.SemaphoreType.DMA((4,)),
            pltpu.SemaphoreType.DMA((8,)),
            pltpu.SemaphoreType.DMA((16,)),
            pltpu.SemaphoreType.DMA((4,)),
            pltpu.SemaphoreType.DMA((4, 4)),
            pltpu.SemaphoreType.DMA((6,)),
        ],
        compiler_params=pltpu.CompilerParams(
            collective_id=0, has_side_effects=True, vmem_limit_bytes=60 * 2**20
        ),
    )(embeddings, labels, landmarks, coeffs, widths[None, :])
    return pl.pallas_call(
        place_kernel,
        out_shape=out_shape,
        in_specs=[anywhere] * 3,
        out_specs=(anywhere,) * 3,
        scratch_shapes=[pltpu.SemaphoreType.DMA((3,))],
        compiler_params=pltpu.CompilerParams(vmem_limit_bytes=60 * 2**20),
    )(*results)


def fits_fused(mesh):
    return mesh.shape["blk"] == 16 and mesh.shape["col"] == 2


def solution(mesh):
    return jax.shard_map(
        fused if fits_fused(mesh) else local,
        mesh=mesh,
        in_specs=(
            P("blk", None),
            P("blk"),
            P(("blk", "col"), None),
            P(("blk", "col"), None),
            P(("blk", "col")),
        ),
        out_specs=(P(("blk", "col"), None), P(("blk", "col"), None), P(("blk", "col"), None)),
        check_vma=False,
    )
```

```python
import functools

import jax
import jax.numpy as jnp
from jax import lax
from jax.experimental import pallas as pl
from jax.experimental.pallas import tpu as pltpu
from jax.sharding import PartitionSpec as P


def from_behind(block, axis, distance):
    devices = range(lax.axis_size(axis))
    route = [((i - distance) % len(devices), i) for i in devices]
    return lax.ppermute(block, axis, route)


def block_kernel(rows, rows_sq, land, width):
    cross = lax.dot_general(
        land, rows, (((1,), (1,)), ((), ())), preferred_element_type=jnp.float32
    )
    land_sq = jnp.sum(jnp.square(land.astype(jnp.float32)), axis=1)
    dist = rows_sq[None, :] + land_sq[:, None] - 2.0 * cross
    return jnp.exp(-width.astype(jnp.float32)[:, None] * dist).astype(jnp.bfloat16)


def class_logits(kern_t, coef):
    return lax.dot_general(
        kern_t, coef, (((0,), (0,)), ((), ())), preferred_element_type=jnp.float32
    )


def logit_gradient(logits, labels):
    top = jnp.max(logits, axis=1, keepdims=True)
    expo = jnp.exp(logits - top)
    probs = expo / jnp.sum(expo, axis=1, keepdims=True)
    classes = lax.broadcasted_iota(jnp.int32, logits.shape, 1)
    onehot = (classes == labels[:, None]).astype(jnp.float32)
    return (probs - onehot).astype(jnp.bfloat16)


def grad_terms(land, coef, width, kern_t, rows, grad_rows):
    grad_kernel = lax.dot_general(
        coef, grad_rows, (((1,), (1,)), ((), ())), preferred_element_type=jnp.float32
    )
    pull = (
        2.0 * width.astype(jnp.float32)[:, None] * grad_kernel * kern_t.astype(jnp.float32)
    ).astype(jnp.bfloat16)
    grad_coef = jnp.dot(kern_t, grad_rows, preferred_element_type=jnp.float32)
    grad_land = jnp.dot(pull, rows, preferred_element_type=jnp.float32) - jnp.sum(
        pull.astype(jnp.float32), axis=1
    )[:, None] * land.astype(jnp.float32)
    return (grad_land, grad_coef, pull)


def project_rows(pull, land):
    return lax.dot_general(pull, land, (((0,), (0,)), ((), ())), preferred_element_type=jnp.float32)


def target_block(position, step, blocks):
    return (position - step - 1) % blocks


def local(embeddings, labels, landmarks, coeffs, widths):
    rows_sq = jnp.sum(jnp.square(embeddings.astype(jnp.float32)), axis=1)
    width_d = embeddings.shape[1]
    classes = coeffs.shape[1]
    size_b = landmarks.shape[0]
    blocks = lax.axis_size("blk")
    position = lax.axis_index("blk")
    all_land, all_coef, all_width = (
        lax.all_gather(landmarks, "blk", axis=0, tiled=True),
        lax.all_gather(coeffs, "blk", axis=0, tiled=True),
        lax.all_gather(widths, "blk", axis=0, tiled=True),
    )
    kern_all = block_kernel(embeddings, rows_sq, all_land, all_width)
    partial_value = class_logits(kern_all, all_coef)
    logits = lax.psum(partial_value, "col")
    grad_rows = logit_gradient(logits, labels)
    sections = ((True, 0, size_b),)

    def pass_on(values):
        return from_behind((values[0], values[1]), "blk", 1)

    empty = tuple(
        (
            (jnp.zeros((size, width_d), jnp.float32), jnp.zeros((size, classes), jnp.float32))
            for upward, low, size in sections
        )
    )
    land_all, coef_all, pull_all = grad_terms(
        all_land, all_coef, all_width, kern_all, embeddings, grad_rows
    )
    pull_z = project_rows(pull_all, all_land)
    pull_rows = jnp.sum(pull_all.astype(jnp.float32), axis=0)

    def select(values, block, low, size):
        return lax.dynamic_slice_in_dim(values, block * size_b + low, size, 0)

    def cached_step(step, accums):
        moved = []
        for index, (upward, low, size) in enumerate(sections):
            block = target_block(position, step, blocks)
            total = (
                accums[index][0] + select(land_all, block, low, size),
                accums[index][1] + select(coef_all, block, low, size),
            )
            moved.append(pass_on(total))
        return tuple(moved)

    accums = lax.fori_loop(0, blocks - 1, cached_step, empty)
    finals = [
        (
            accums[index][0] + select(land_all, position, low, size),
            accums[index][1] + select(coef_all, position, low, size),
        )
        for index, (upward, low, size) in enumerate(sections)
    ]
    grad_landmarks = jnp.concatenate([item[0] for item in finals], axis=0)
    grad_coeffs = jnp.concatenate([item[1] for item in finals], axis=0)
    local_rows = pull_z - pull_rows[:, None] * embeddings.astype(jnp.float32)
    grad_embeddings = lax.psum_scatter(local_rows, "col", scatter_dimension=0, tiled=True)
    return (grad_landmarks, grad_coeffs, grad_embeddings)


NT = (((1,), (1,)), ((), ()))
TN = (((0,), (0,)), ((), ()))


def fused_kernel(
    classes, emb_hbm, lab_hbm, land_hbm, coef_hbm, width_hbm,
    out_land, out_coef, out_emb,
    emb, lab_ref, land_ref, coef_ref, width_ref,
    table, kern, pull, pull_t, logits, grad, acc, emb_out,
    to_core, from_core, to_second, from_second, to_first, from_first, to_z, from_z,
    send_sem, z_sem, first_sem, second_sem, core_sem, back_sem, piece_sem, back_z_sem, local_sem,
):
    blk, col = lax.axis_index("blk"), lax.axis_index("col")
    size, depth = land_ref.shape
    wide = table.shape[1]
    rows = emb.shape[0]
    slab, half = 4 * size, 8 * size
    other = 1 - col
    x, y, z = blk % 2, (blk // 2) % 2, blk // 4
    my1 = x * other + y * col
    my2 = y * other + x * col
    first = (blk + (1 - 2 * my1) * (1 + col), col)
    second = (blk + (1 - 2 * my2) * (2 - col), col)
    core = (blk, other)
    far = z // 2
    toward = 1 - 2 * far
    within = z + far * (3 - 2 * z)
    nearest = [3 * far + toward * at for at in (1 - within, 2, 3)]

    def at_z(where):
        return where * 4 + blk % 4, col

    def base(c, p2, p1):
        return ((c * 2 + p2) * 2 + p1) * slab

    def piece(start, where):
        return pl.ds(pl.multiple_of(start + where * size, size), size)

    mine = emb_hbm.at[pl.ds(pl.multiple_of(col * rows, 64), rows)]
    loads = [
        pltpu.make_async_copy(src, dst, local_sem.at[n])
        for n, (src, dst) in enumerate((
            (land_hbm, land_ref), (coef_hbm, coef_ref), (width_hbm, width_ref),
            (lab_hbm, lab_ref), (mine, emb),
        ))
    ]
    for load in loads:
        load.start()

    barrier = pltpu.get_barrier_semaphore()
    peers = [first, second, core] + [at_z(where) for where in nearest]
    for peer in peers:
        pl.semaphore_signal(barrier, inc=1, device_id=peer, device_id_type=pl.DeviceIdType.MESH)

    own = piece(base(col, my2, my1), z)
    for load in loads[:3]:
        load.wait()
    eye = lax.broadcasted_iota(jnp.int32, (size, size), 0) == lax.broadcasted_iota(
        jnp.int32, (size, size), 1
    )
    width_col = jnp.sum(
        jnp.where(eye, width_ref[...].astype(jnp.float32), 0.0), axis=1, keepdims=True
    )
    tail = wide - 128
    split = tail - depth
    lanes = lax.broadcasted_iota(jnp.int32, (size, 128), 1)
    last = jnp.concatenate(
        [
            coef_ref[:, split:].astype(jnp.float32),
            jnp.zeros((size, 128 - (classes - split)), jnp.float32),
        ],
        axis=1,
    )
    last = jnp.where(lanes == classes - split, width_col, last)
    table[own, :depth] = land_ref[...]
    table[own, depth:tail] = coef_ref[:, :split]
    table[own, tail:] = last.astype(jnp.bfloat16)

    pl.semaphore_wait(barrier, len(peers))

    sends = []

    def send(src, dst, recv, device):
        copy = pltpu.make_async_remote_copy(
            src_ref=src, dst_ref=dst, send_sem=send_sem.at[len(sends)], recv_sem=recv,
            device_id=device, device_id_type=pl.DeviceIdType.MESH,
        )
        copy.start()
        sends.append(copy)

    def arrived(dst, recv):
        pltpu.make_async_remote_copy(
            src_ref=dst, dst_ref=dst, send_sem=send_sem.at[0], recv_sem=recv,
            device_id=core, device_id_type=pl.DeviceIdType.MESH,
        ).wait_recv()

    def put(where, recv, device):
        send(table.at[where], table.at[where], recv, device)

    slab_a = base(col, my2, my1)
    slab_b = base(col, my2, 1 - my1)
    slab_c = base(col, 1 - my2, my1)
    slab_d = base(col, 1 - my2, 1 - my1)
    for where in nearest:
        put(own, z_sem.at[z], at_z(where))
    put(own, second_sem.at[0], second)
    put(own, first_sem.at[0], first)
    put(own, core_sem.at[0], core)

    for load in loads[3:]:
        load.wait()
    emb_f = emb[...].astype(jnp.float32)
    eye_rows = lax.broadcasted_iota(jnp.int32, (rows, rows), 0) == lax.broadcasted_iota(
        jnp.int32, (rows, rows), 1
    )
    rows_sq = jnp.sum(jnp.square(emb_f), axis=1, keepdims=True)
    rows_sq = jnp.sum(jnp.where(eye_rows, rows_sq, 0.0), axis=0, keepdims=True)

    around = [z] + nearest
    for k in (1, 2, 3):
        where = piece(slab_a, around[k])
        arrived(table.at[where], z_sem.at[around[k]])
        put(where, first_sem.at[k], first)
        put(where, second_sem.at[k], second)
        put(where, core_sem.at[k], core)

    def widths_of(where):
        end = table[where, tail:].astype(jnp.float32)
        at = lax.broadcasted_iota(jnp.int32, end.shape, 1) == classes - split
        return jnp.sum(jnp.where(at, end, 0.0), axis=1, keepdims=True)

    def forward(start, fresh):
        where = pl.ds(pl.multiple_of(start, half), half)
        land = table[where, :depth]
        cross = lax.dot_general(land, emb[...], NT, preferred_element_type=jnp.float32)
        land_sq = jnp.sum(jnp.square(land.astype(jnp.float32)), axis=1, keepdims=True)
        dist = (rows_sq + land_sq) - 2.0 * cross
        value = jnp.exp(-widths_of(where) * dist).astype(jnp.bfloat16)
        kern[where, :] = value
        part = lax.dot_general(
            value, table[where, depth:], TN, preferred_element_type=jnp.float32
        )
        if fresh:
            logits[...] = part
        else:
            logits[...] += part

    for k in range(4):
        where = piece(slab_b, around[k])
        arrived(table.at[where], first_sem.at[k])
        put(where, second_sem.at[4 + k], second)
        put(where, core_sem.at[4 + k], core)
    forward(base(col, my2, 0), True)
    for n, start in enumerate((base(other, my1, my2), base(other, my1, 1 - my2))):
        for k in range(4):
            arrived(table.at[piece(start, around[k])], core_sem.at[4 * n + k])
    forward(base(other, my1, 0), False)
    for n, start in enumerate((slab_c, slab_d)):
        for k in range(4):
            where = piece(start, around[k])
            arrived(table.at[where], second_sem.at[4 * n + k])
            put(where, core_sem.at[8 + 4 * n + k], core)
    forward(base(col, 1 - my2, 0), False)
    for n, start in enumerate((base(other, 1 - my1, my2), base(other, 1 - my1, 1 - my2))):
        for k in range(4):
            arrived(table.at[piece(start, around[k])], core_sem.at[8 + 4 * n + k])
    forward(base(other, 1 - my1, 0), False)

    all_rows = lab_ref.shape[0]
    mine = lax.broadcasted_iota(jnp.int32, (rows, all_rows), 1) == (
        lax.broadcasted_iota(jnp.int32, (rows, all_rows), 0) + col * rows
    )
    label = jnp.sum(
        jnp.where(mine, lab_ref[...].astype(jnp.float32)[None, :], 0.0), axis=1, keepdims=True
    ).astype(jnp.int32)
    place = lax.broadcasted_iota(jnp.int32, logits.shape, 1)
    value = jnp.where(place < classes, logits[...], -jnp.inf)
    expo = jnp.exp(value - jnp.max(value, axis=1, keepdims=True))
    probs = expo / jnp.sum(expo, axis=1, keepdims=True)
    grad[...] = (probs - jnp.where(place == label, 1.0, 0.0)).astype(jnp.bfloat16)

    def terms(start):
        where = pl.ds(pl.multiple_of(start, half), half)
        grad_kernel = lax.dot_general(
            table[where, depth:], grad[...], NT, preferred_element_type=jnp.float32
        )
        tug = (
            2.0 * widths_of(where) * grad_kernel * kern[where, :].astype(jnp.float32)
        ).astype(jnp.bfloat16)
        pull[where, :] = tug
        land = jnp.dot(tug, emb[...], preferred_element_type=jnp.float32)
        land -= jnp.sum(tug.astype(jnp.float32), axis=1, keepdims=True) * table[
            where, :depth
        ].astype(jnp.float32)
        coef = jnp.dot(kern[where, :], grad[...], preferred_element_type=jnp.float32)
        return land, coef

    def part(index):
        return pl.ds(pl.multiple_of(index * slab, slab), slab)

    def for_core(n, p2):
        land, coef = terms(base(other, p2, 0))
        to_core[n, :, :depth] = land.astype(jnp.bfloat16)
        to_core[n, :, depth:] = coef.astype(jnp.bfloat16)
        for m, p1 in enumerate((1 - my2, my2)):
            send(
                to_core.at[n, part(p1)], from_core.at[n, part(p1)],
                back_sem.at[2 * n + m], core,
            )

    def for_self(n, p2):
        land, coef = terms(base(col, p2, 0))
        acc[n, :, :depth] = land
        acc[n, :, depth:] = coef

    def target(p1, where):
        start = p1 * slab + where * size
        return pl.ds(pl.multiple_of(start, size), size)

    order = around[::-1]
    for_core(0, 1 - my1)
    for_self(0, 1 - my2)
    for m, p1 in enumerate((1 - my1, my1)):
        arrived(from_core.at[0, part(p1)], back_sem.at[m])
    for n, k in enumerate(order):
        for m, p1 in enumerate((1 - my1, my1)):
            where = target(p1, k)
            total = acc[0, where, :] + from_core[0, where, :].astype(jnp.float32)
            to_second[n, m] = total.astype(jnp.bfloat16)
            send(to_second.at[n, m], from_second.at[n, m], piece_sem.at[n, m], second)
    for_core(1, my1)
    for_self(1, my2)
    for m, p1 in enumerate((1 - my1, my1)):
        arrived(from_core.at[1, part(p1)], back_sem.at[2 + m])

    def summed(n, m, p1, k):
        where = target(p1, k)
        arrived(from_second.at[n, m], piece_sem.at[n, m])
        return (
            acc[1, where, :]
            + from_core[1, where, :].astype(jnp.float32)
            + from_second[n, m].astype(jnp.float32)
        )

    def pass_first(n):
        to_first[n] = summed(n, 0, 1 - my1, order[n]).astype(jnp.bfloat16)
        send(to_first.at[n], from_first.at[n], piece_sem.at[n, 2], first)

    def collect(n):
        total = summed(n, 1, my1, order[n])
        arrived(from_first.at[n], piece_sem.at[n, 2])
        return total + from_first[n].astype(jnp.float32)

    def pass_z(n):
        to_z[n] = collect(n).astype(jnp.bfloat16)
        send(to_z.at[n], from_z.at[z], back_z_sem.at[z], at_z(order[n]))

    def project(n):
        where = pl.ds(n * slab, slab)
        tug = pull_t[where, :]
        drawn = jnp.dot(tug, table[:, :depth], preferred_element_type=jnp.float32)
        emb_out[where, :] = drawn - jnp.sum(
            tug.astype(jnp.float32), axis=1, keepdims=True
        ) * emb[where, :].astype(jnp.float32)

    pull_t[...] = pull[...].T
    pass_first(0)
    project(0)
    pass_first(1)
    pass_z(0)
    project(1)
    pass_first(2)
    pass_z(1)
    project(2)
    store = pltpu.make_async_copy(emb_out, out_emb, local_sem.at[5])
    store.start()
    pass_first(3)
    pass_z(2)
    result = collect(3)
    for where in order[:3]:
        arrived(from_z.at[where], back_z_sem.at[where])
        result += from_z[where].astype(jnp.float32)
    out_land[...] = result[:, :depth]
    out_coef[...] = result[:, depth : depth + classes]

    store.wait()
    for copy in sends:
        copy.wait_send()


def place_kernel(emb, coef, land, out_emb, out_coef, out_land, held_emb, held_coef, held_land, sem):
    held = (held_emb, held_coef, held_land)
    loads = [
        pltpu.make_async_copy(src, dst, sem.at[0, n])
        for n, (src, dst) in enumerate(zip((emb, coef, land), held))
    ]
    stores = [
        pltpu.make_async_copy(src, dst, sem.at[1, n])
        for n, (src, dst) in enumerate(zip(held, (out_emb, out_coef, out_land)))
    ]
    for load in loads:
        load.start()
    for load, store in zip(loads, stores):
        load.wait()
        store.start()
    for store in stores:
        store.wait()


def fused(embeddings, labels, landmarks, coeffs, widths):
    size, depth = landmarks.shape
    classes = coeffs.shape[1]
    rows = embeddings.shape[0] // 2
    padded = (classes // 128 + 1) * 128
    wide = depth + padded
    count, half = 32 * size, 8 * size
    vmem = pl.BlockSpec(memory_space=pltpu.VMEM)
    hbm = pl.BlockSpec(memory_space=pltpu.HBM)
    anywhere = pl.BlockSpec(memory_space=pl.ANY)
    bf16, f32 = jnp.bfloat16, jnp.float32
    out_shape = (
        jax.ShapeDtypeStruct((size, depth), f32),
        jax.ShapeDtypeStruct((size, classes), f32),
        jax.ShapeDtypeStruct((rows, depth), f32),
    )
    results = pl.pallas_call(
        functools.partial(fused_kernel, classes),
        out_shape=out_shape,
        in_specs=[hbm] * 5,
        out_specs=(vmem, vmem, anywhere),
        scratch_shapes=[
            pltpu.VMEM((rows, depth), bf16),
            pltpu.VMEM(labels.shape, labels.dtype),
            pltpu.VMEM(landmarks.shape, bf16),
            pltpu.VMEM(coeffs.shape, bf16),
            pltpu.VMEM((1, size), bf16),
            pltpu.VMEM((count, wide), bf16),
            pltpu.VMEM((count, rows), bf16),
            pltpu.VMEM((count, rows), bf16),
            pltpu.VMEM((rows, count), bf16),
            pltpu.VMEM((rows, padded), f32),
            pltpu.VMEM((rows, padded), bf16),
            pltpu.VMEM((2, half, wide), f32),
            pltpu.VMEM((rows, depth), f32),
            pltpu.VMEM((2, half, wide), bf16),
            pltpu.VMEM((2, half, wide), bf16),
            pltpu.VMEM((4, 2, size, wide), bf16),
            pltpu.VMEM((4, 2, size, wide), bf16),
            pltpu.VMEM((4, size, wide), bf16),
            pltpu.VMEM((4, size, wide), bf16),
            pltpu.VMEM((3, size, wide), bf16),
            pltpu.VMEM((4, size, wide), bf16),
            pltpu.SemaphoreType.DMA((50,)),
            pltpu.SemaphoreType.DMA((4,)),
            pltpu.SemaphoreType.DMA((4,)),
            pltpu.SemaphoreType.DMA((8,)),
            pltpu.SemaphoreType.DMA((16,)),
            pltpu.SemaphoreType.DMA((4,)),
            pltpu.SemaphoreType.DMA((4, 3)),
            pltpu.SemaphoreType.DMA((4,)),
            pltpu.SemaphoreType.DMA((6,)),
        ],
        compiler_params=pltpu.CompilerParams(
            collective_id=0, has_side_effects=True, vmem_limit_bytes=60 * 2**20
        ),
    )(embeddings, labels, landmarks, coeffs, widths[None, :])
    grad_emb, grad_coef, grad_land = pl.pallas_call(
        place_kernel,
        out_shape=out_shape[::-1],
        in_specs=[anywhere] * 3,
        out_specs=(anywhere,) * 3,
        scratch_shapes=[pltpu.VMEM(out.shape, out.dtype) for out in out_shape[::-1]]
        + [pltpu.SemaphoreType.DMA((2, 3))],
        compiler_params=pltpu.CompilerParams(vmem_limit_bytes=60 * 2**20),
    )(*results[::-1])
    return grad_land, grad_coef, grad_emb


def fits_fused(mesh):
    return mesh.shape["blk"] == 16 and mesh.shape["col"] == 2


def solution(mesh):
    return jax.shard_map(
        fused if fits_fused(mesh) else local,
        mesh=mesh,
        in_specs=(
            P("blk", None),
            P("blk"),
            P(("blk", "col"), None),
            P(("blk", "col"), None),
            P(("blk", "col")),
        ),
        out_specs=(P(("blk", "col"), None), P(("blk", "col"), None), P(("blk", "col"), None)),
        check_vma=False,
    )
```

```python
import functools

import jax
import jax.numpy as jnp
from jax import lax
from jax.experimental import pallas as pl
from jax.experimental.pallas import tpu as pltpu
from jax.sharding import PartitionSpec as P


def from_behind(block, axis, distance):
    devices = range(lax.axis_size(axis))
    route = [((i - distance) % len(devices), i) for i in devices]
    return lax.ppermute(block, axis, route)


def block_kernel(rows, rows_sq, land, width):
    cross = lax.dot_general(
        land, rows, (((1,), (1,)), ((), ())), preferred_element_type=jnp.float32
    )
    land_sq = jnp.sum(jnp.square(land.astype(jnp.float32)), axis=1)
    dist = rows_sq[None, :] + land_sq[:, None] - 2.0 * cross
    return jnp.exp(-width.astype(jnp.float32)[:, None] * dist).astype(jnp.bfloat16)


def class_logits(kern_t, coef):
    return lax.dot_general(
        kern_t, coef, (((0,), (0,)), ((), ())), preferred_element_type=jnp.float32
    )


def logit_gradient(logits, labels):
    top = jnp.max(logits, axis=1, keepdims=True)
    expo = jnp.exp(logits - top)
    probs = expo / jnp.sum(expo, axis=1, keepdims=True)
    classes = lax.broadcasted_iota(jnp.int32, logits.shape, 1)
    onehot = (classes == labels[:, None]).astype(jnp.float32)
    return (probs - onehot).astype(jnp.bfloat16)


def grad_terms(land, coef, width, kern_t, rows, grad_rows):
    grad_kernel = lax.dot_general(
        coef, grad_rows, (((1,), (1,)), ((), ())), preferred_element_type=jnp.float32
    )
    pull = (
        2.0 * width.astype(jnp.float32)[:, None] * grad_kernel * kern_t.astype(jnp.float32)
    ).astype(jnp.bfloat16)
    grad_coef = jnp.dot(kern_t, grad_rows, preferred_element_type=jnp.float32)
    grad_land = jnp.dot(pull, rows, preferred_element_type=jnp.float32) - jnp.sum(
        pull.astype(jnp.float32), axis=1
    )[:, None] * land.astype(jnp.float32)
    return (grad_land, grad_coef, pull)


def project_rows(pull, land):
    return lax.dot_general(pull, land, (((0,), (0,)), ((), ())), preferred_element_type=jnp.float32)


def target_block(position, step, blocks):
    return (position - step - 1) % blocks


def local(embeddings, labels, landmarks, coeffs, widths):
    rows_sq = jnp.sum(jnp.square(embeddings.astype(jnp.float32)), axis=1)
    width_d = embeddings.shape[1]
    classes = coeffs.shape[1]
    size_b = landmarks.shape[0]
    blocks = lax.axis_size("blk")
    position = lax.axis_index("blk")
    all_land, all_coef, all_width = (
        lax.all_gather(landmarks, "blk", axis=0, tiled=True),
        lax.all_gather(coeffs, "blk", axis=0, tiled=True),
        lax.all_gather(widths, "blk", axis=0, tiled=True),
    )
    kern_all = block_kernel(embeddings, rows_sq, all_land, all_width)
    partial_value = class_logits(kern_all, all_coef)
    logits = lax.psum(partial_value, "col")
    grad_rows = logit_gradient(logits, labels)
    sections = ((True, 0, size_b),)

    def pass_on(values):
        return from_behind((values[0], values[1]), "blk", 1)

    empty = tuple(
        (
            (jnp.zeros((size, width_d), jnp.float32), jnp.zeros((size, classes), jnp.float32))
            for upward, low, size in sections
        )
    )
    land_all, coef_all, pull_all = grad_terms(
        all_land, all_coef, all_width, kern_all, embeddings, grad_rows
    )
    pull_z = project_rows(pull_all, all_land)
    pull_rows = jnp.sum(pull_all.astype(jnp.float32), axis=0)

    def select(values, block, low, size):
        return lax.dynamic_slice_in_dim(values, block * size_b + low, size, 0)

    def cached_step(step, accums):
        moved = []
        for index, (upward, low, size) in enumerate(sections):
            block = target_block(position, step, blocks)
            total = (
                accums[index][0] + select(land_all, block, low, size),
                accums[index][1] + select(coef_all, block, low, size),
            )
            moved.append(pass_on(total))
        return tuple(moved)

    accums = lax.fori_loop(0, blocks - 1, cached_step, empty)
    finals = [
        (
            accums[index][0] + select(land_all, position, low, size),
            accums[index][1] + select(coef_all, position, low, size),
        )
        for index, (upward, low, size) in enumerate(sections)
    ]
    grad_landmarks = jnp.concatenate([item[0] for item in finals], axis=0)
    grad_coeffs = jnp.concatenate([item[1] for item in finals], axis=0)
    local_rows = pull_z - pull_rows[:, None] * embeddings.astype(jnp.float32)
    grad_embeddings = lax.psum_scatter(local_rows, "col", scatter_dimension=0, tiled=True)
    return (grad_landmarks, grad_coeffs, grad_embeddings)


NT = (((1,), (1,)), ((), ()))
TN = (((0,), (0,)), ((), ()))


def fused_kernel(
    classes, emb_hbm, lab_hbm, land_hbm, coef_hbm, width_hbm,
    out_land, out_coef, out_emb,
    emb, lab_ref, land_ref, coef_ref, width_ref,
    table, kern, pull, pull_t, logits, grad, acc,
    to_core, from_core, to_second, from_second, to_first, from_first, to_z, from_z,
    send_sem, z_sem, first_sem, second_sem, core_sem, back_sem, piece_sem, back_z_sem, pair_sem, local_sem,
):
    blk, col = lax.axis_index("blk"), lax.axis_index("col")
    size, depth = land_ref.shape
    wide = table.shape[1]
    rows = emb.shape[0]
    slab, half = 4 * size, 8 * size
    other = 1 - col
    x, y, z = blk % 2, (blk // 2) % 2, blk // 4
    my1 = x * other + y * col
    my2 = y * other + x * col
    first = (blk + (1 - 2 * my1) * (1 + col), col)
    second = (blk + (1 - 2 * my2) * (2 - col), col)
    core = (blk, other)
    far = z // 2
    toward = 1 - 2 * far
    within = z + far * (3 - 2 * z)
    nearest = [3 * far + toward * at for at in (1 - within, 2, 3)]

    def at_z(where):
        return where * 4 + blk % 4, col

    def base(c, p2, p1):
        return ((c * 2 + p2) * 2 + p1) * slab

    def piece(start, where):
        return pl.ds(pl.multiple_of(start + where * size, size), size)

    mine = emb_hbm.at[pl.ds(pl.multiple_of(col * rows, 64), rows)]
    loads = [
        pltpu.make_async_copy(src, dst, local_sem.at[n])
        for n, (src, dst) in enumerate((
            (land_hbm, land_ref), (coef_hbm, coef_ref), (width_hbm, width_ref),
            (lab_hbm, lab_ref), (mine, emb),
        ))
    ]
    for load in loads:
        load.start()

    barrier = pltpu.get_barrier_semaphore()
    peers = [first, second, core] + [at_z(where) for where in nearest]
    for peer in peers:
        pl.semaphore_signal(barrier, inc=1, device_id=peer, device_id_type=pl.DeviceIdType.MESH)

    own = piece(base(col, my2, my1), z)
    for load in loads[:3]:
        load.wait()
    eye = lax.broadcasted_iota(jnp.int32, (size, size), 0) == lax.broadcasted_iota(
        jnp.int32, (size, size), 1
    )
    width_col = jnp.sum(
        jnp.where(eye, width_ref[...].astype(jnp.float32), 0.0), axis=1, keepdims=True
    )
    tail = wide - 128
    split = tail - depth
    lanes = lax.broadcasted_iota(jnp.int32, (size, 128), 1)
    last = jnp.concatenate(
        [
            coef_ref[:, split:].astype(jnp.float32),
            jnp.zeros((size, 128 - (classes - split)), jnp.float32),
        ],
        axis=1,
    )
    last = jnp.where(lanes == classes - split, width_col, last)
    table[own, :depth] = land_ref[...]
    table[own, depth:tail] = coef_ref[:, :split]
    table[own, tail:] = last.astype(jnp.bfloat16)

    pl.semaphore_wait(barrier, len(peers))

    sends = []

    def send(src, dst, recv, device):
        copy = pltpu.make_async_remote_copy(
            src_ref=src, dst_ref=dst, send_sem=send_sem.at[len(sends)], recv_sem=recv,
            device_id=device, device_id_type=pl.DeviceIdType.MESH,
        )
        copy.start()
        sends.append(copy)

    def arrived(dst, recv):
        pltpu.make_async_remote_copy(
            src_ref=dst, dst_ref=dst, send_sem=send_sem.at[0], recv_sem=recv,
            device_id=core, device_id_type=pl.DeviceIdType.MESH,
        ).wait_recv()

    def put(where, recv, device):
        send(table.at[where], table.at[where], recv, device)

    slab_a = base(col, my2, my1)
    slab_b = base(col, my2, 1 - my1)
    slab_c = base(col, 1 - my2, my1)
    slab_d = base(col, 1 - my2, 1 - my1)
    for where in nearest:
        put(own, z_sem.at[z], at_z(where))
    put(own, second_sem.at[0], second)
    put(own, first_sem.at[0], first)
    put(own, core_sem.at[0], core)

    for load in loads[3:]:
        load.wait()
    emb_f = emb[...].astype(jnp.float32)
    eye_rows = lax.broadcasted_iota(jnp.int32, (rows, rows), 0) == lax.broadcasted_iota(
        jnp.int32, (rows, rows), 1
    )
    rows_sq = jnp.sum(jnp.square(emb_f), axis=1, keepdims=True)
    rows_sq = jnp.sum(jnp.where(eye_rows, rows_sq, 0.0), axis=0, keepdims=True)

    around = [z] + nearest
    for k in (1, 2, 3):
        where = piece(slab_a, around[k])
        arrived(table.at[where], z_sem.at[around[k]])
        put(where, first_sem.at[k], first)
        if k != 1:
            put(where, second_sem.at[k], second)
        put(where, core_sem.at[k], core)

    def widths_of(where):
        end = table[where, tail:].astype(jnp.float32)
        at = lax.broadcasted_iota(jnp.int32, end.shape, 1) == classes - split
        return jnp.sum(jnp.where(at, end, 0.0), axis=1, keepdims=True)

    def forward(start, fresh):
        where = pl.ds(pl.multiple_of(start, half), half)
        land = table[where, :depth]
        cross = lax.dot_general(land, emb[...], NT, preferred_element_type=jnp.float32)
        land_sq = jnp.sum(jnp.square(land.astype(jnp.float32)), axis=1, keepdims=True)
        dist = (rows_sq + land_sq) - 2.0 * cross
        value = jnp.exp(-widths_of(where) * dist).astype(jnp.bfloat16)
        kern[where, :] = value
        part = lax.dot_general(
            value, table[where, depth:], TN, preferred_element_type=jnp.float32
        )
        if fresh:
            logits[...] = part
        else:
            logits[...] += part

    for k in range(4):
        where = piece(slab_b, around[k])
        arrived(table.at[where], first_sem.at[k])
        if k != 1:
            put(where, second_sem.at[4 + k], second)
        put(where, core_sem.at[4 + k], core)
    forward(base(col, my2, 0), True)
    for n, start in enumerate((base(other, my1, my2), base(other, my1, 1 - my2))):
        for k in range(4):
            arrived(table.at[piece(start, around[k])], core_sem.at[4 * n + k])
    forward(base(other, my1, 0), False)
    for n, start in enumerate((slab_c, slab_d)):
        for k in (0, 2, 3, 1):
            where = piece(start, around[k])
            arrived(table.at[where], pair_sem.at[n] if k == 1 else second_sem.at[4 * n + k])
            if k == 0:
                put(where, pair_sem.at[n], at_z(around[1]))
            put(where, core_sem.at[8 + 4 * n + k], core)
    forward(base(col, 1 - my2, 0), False)
    for n, start in enumerate((base(other, 1 - my1, my2), base(other, 1 - my1, 1 - my2))):
        for k in range(4):
            arrived(table.at[piece(start, around[k])], core_sem.at[8 + 4 * n + k])
    forward(base(other, 1 - my1, 0), False)

    all_rows = lab_ref.shape[0]
    mine = lax.broadcasted_iota(jnp.int32, (rows, all_rows), 1) == (
        lax.broadcasted_iota(jnp.int32, (rows, all_rows), 0) + col * rows
    )
    label = jnp.sum(
        jnp.where(mine, lab_ref[...].astype(jnp.float32)[None, :], 0.0), axis=1, keepdims=True
    ).astype(jnp.int32)
    place = lax.broadcasted_iota(jnp.int32, logits.shape, 1)
    value = jnp.where(place < classes, logits[...], -jnp.inf)
    expo = jnp.exp(value - jnp.max(value, axis=1, keepdims=True))
    probs = expo / jnp.sum(expo, axis=1, keepdims=True)
    grad[...] = (probs - jnp.where(place == label, 1.0, 0.0)).astype(jnp.bfloat16)

    def terms(start):
        where = pl.ds(pl.multiple_of(start, half), half)
        grad_kernel = lax.dot_general(
            table[where, depth:], grad[...], NT, preferred_element_type=jnp.float32
        )
        tug = (
            2.0 * widths_of(where) * grad_kernel * kern[where, :].astype(jnp.float32)
        ).astype(jnp.bfloat16)
        pull[where, :] = tug
        land = jnp.dot(tug, emb[...], preferred_element_type=jnp.float32)
        land -= jnp.sum(tug.astype(jnp.float32), axis=1, keepdims=True) * table[
            where, :depth
        ].astype(jnp.float32)
        coef = jnp.dot(kern[where, :], grad[...], preferred_element_type=jnp.float32)
        return land, coef

    def part(index):
        return pl.ds(pl.multiple_of(index * slab, slab), slab)

    def for_core(n, p2):
        land, coef = terms(base(other, p2, 0))
        to_core[n, :, :depth] = land.astype(jnp.bfloat16)
        to_core[n, :, depth:] = coef.astype(jnp.bfloat16)
        for m, p1 in enumerate((1 - my2, my2)):
            send(
                to_core.at[n, part(p1)], from_core.at[n, part(p1)],
                back_sem.at[2 * n + m], core,
            )

    def for_self(n, p2):
        land, coef = terms(base(col, p2, 0))
        acc[n, :, :depth] = land
        acc[n, :, depth:] = coef

    def target(p1, where):
        start = p1 * slab + where * size
        return pl.ds(pl.multiple_of(start, size), size)

    order = around[::-1]
    for_core(0, 1 - my1)
    for_self(0, 1 - my2)
    for m, p1 in enumerate((1 - my1, my1)):
        arrived(from_core.at[0, part(p1)], back_sem.at[m])
    for n in (2, 0, 1, 3):
        for m, p1 in enumerate((1 - my1, my1)):
            where = target(p1, order[n])
            total = acc[0, where, :] + from_core[0, where, :].astype(jnp.float32)
            if n == 3:
                arrived(from_second.at[2, m], piece_sem.at[2, m])
                total += from_second[2, m].astype(jnp.float32)
            to_second[n, m] = total.astype(jnp.bfloat16)
            send(
                to_second.at[n, m], from_second.at[n, m], piece_sem.at[n, m],
                at_z(order[2]) if n == 2 else second,
            )
    for_core(1, my1)
    for_self(1, my2)
    for m, p1 in enumerate((1 - my1, my1)):
        arrived(from_core.at[1, part(p1)], back_sem.at[2 + m])

    def summed(n, m, p1, k):
        where = target(p1, k)
        total = acc[1, where, :] + from_core[1, where, :].astype(jnp.float32)
        if n != 2:
            arrived(from_second.at[n, m], piece_sem.at[n, m])
            total += from_second[n, m].astype(jnp.float32)
        return total

    def pass_first(n):
        to_first[n] = summed(n, 0, 1 - my1, order[n]).astype(jnp.bfloat16)
        send(to_first.at[n], from_first.at[n], piece_sem.at[n, 2], first)

    def collect(n):
        total = summed(n, 1, my1, order[n])
        arrived(from_first.at[n], piece_sem.at[n, 2])
        return total + from_first[n].astype(jnp.float32)

    def pass_z(n):
        to_z[n] = collect(n).astype(jnp.bfloat16)
        send(to_z.at[n], from_z.at[z], back_z_sem.at[z], at_z(order[n]))

    def project(n):
        where = pl.ds(n * slab, slab)
        tug = pull_t[where, :]
        drawn = jnp.dot(tug, table[:, :depth], preferred_element_type=jnp.float32)
        out_emb[where, :] = drawn - jnp.sum(
            tug.astype(jnp.float32), axis=1, keepdims=True
        ) * emb[where, :].astype(jnp.float32)

    pull_t[...] = pull[...].T
    pass_first(0)
    project(0)
    pass_first(1)
    pass_z(0)
    project(1)
    pass_first(2)
    pass_z(1)
    project(2)
    pass_first(3)
    pass_z(2)
    result = collect(3)
    for where in order[:3]:
        arrived(from_z.at[where], back_z_sem.at[where])
        result += from_z[where].astype(jnp.float32)
    out_land[...] = result[:, :depth]
    out_coef[...] = result[:, depth : depth + classes]

    for copy in sends:
        copy.wait_send()


def place_kernel(emb, coef, land, out_emb, out_coef, out_land, sem):
    stores = [
        pltpu.make_async_copy(src, dst, sem.at[n])
        for n, (src, dst) in enumerate(((emb, out_emb), (coef, out_coef), (land, out_land)))
    ]
    for store in stores:
        store.start()
    for store in stores:
        store.wait()


def fused(embeddings, labels, landmarks, coeffs, widths):
    size, depth = landmarks.shape
    classes = coeffs.shape[1]
    rows = embeddings.shape[0] // 2
    padded = (classes // 128 + 1) * 128
    wide = depth + padded
    count, half = 32 * size, 8 * size
    vmem = pl.BlockSpec(memory_space=pltpu.VMEM)
    hbm = pl.BlockSpec(memory_space=pltpu.HBM)
    anywhere = pl.BlockSpec(memory_space=pl.ANY)
    bf16, f32 = jnp.bfloat16, jnp.float32
    out_shape = (
        jax.ShapeDtypeStruct((size, depth), f32),
        jax.ShapeDtypeStruct((size, classes), f32),
        jax.ShapeDtypeStruct((rows, depth), f32),
    )
    results = pl.pallas_call(
        functools.partial(fused_kernel, classes),
        out_shape=tuple(pltpu.VMEM(out.shape, out.dtype) for out in out_shape),
        in_specs=[hbm] * 5,
        out_specs=(vmem,) * 3,
        scratch_shapes=[
            pltpu.VMEM((rows, depth), bf16),
            pltpu.VMEM(labels.shape, labels.dtype),
            pltpu.VMEM(landmarks.shape, bf16),
            pltpu.VMEM(coeffs.shape, bf16),
            pltpu.VMEM((1, size), bf16),
            pltpu.VMEM((count, wide), bf16),
            pltpu.VMEM((count, rows), bf16),
            pltpu.VMEM((count, rows), bf16),
            pltpu.VMEM((rows, count), bf16),
            pltpu.VMEM((rows, padded), f32),
            pltpu.VMEM((rows, padded), bf16),
            pltpu.VMEM((2, half, wide), f32),
            pltpu.VMEM((2, half, wide), bf16),
            pltpu.VMEM((2, half, wide), bf16),
            pltpu.VMEM((4, 2, size, wide), bf16),
            pltpu.VMEM((4, 2, size, wide), bf16),
            pltpu.VMEM((4, size, wide), bf16),
            pltpu.VMEM((4, size, wide), bf16),
            pltpu.VMEM((3, size, wide), bf16),
            pltpu.VMEM((4, size, wide), bf16),
            pltpu.SemaphoreType.DMA((50,)),
            pltpu.SemaphoreType.DMA((4,)),
            pltpu.SemaphoreType.DMA((4,)),
            pltpu.SemaphoreType.DMA((8,)),
            pltpu.SemaphoreType.DMA((16,)),
            pltpu.SemaphoreType.DMA((4,)),
            pltpu.SemaphoreType.DMA((4, 3)),
            pltpu.SemaphoreType.DMA((4,)),
            pltpu.SemaphoreType.DMA((2,)),
            pltpu.SemaphoreType.DMA((5,)),
        ],
        compiler_params=pltpu.CompilerParams(
            collective_id=0, has_side_effects=True, vmem_limit_bytes=60 * 2**20
        ),
    )(embeddings, labels, landmarks, coeffs, widths[None, :])
    grad_emb, grad_coef, grad_land = pl.pallas_call(
        place_kernel,
        out_shape=out_shape[::-1],
        in_specs=[vmem] * 3,
        out_specs=(anywhere,) * 3,
        scratch_shapes=[pltpu.SemaphoreType.DMA((3,))],
        compiler_params=pltpu.CompilerParams(vmem_limit_bytes=16 * 2**20),
    )(*results[::-1])
    return grad_land, grad_coef, grad_emb


def fits_fused(mesh):
    return mesh.shape["blk"] == 16 and mesh.shape["col"] == 2


def solution(mesh):
    return jax.shard_map(
        fused if fits_fused(mesh) else local,
        mesh=mesh,
        in_specs=(
            P("blk", None),
            P("blk"),
            P(("blk", "col"), None),
            P(("blk", "col"), None),
            P(("blk", "col")),
        ),
        out_specs=(P(("blk", "col"), None), P(("blk", "col"), None), P(("blk", "col"), None)),
        check_vma=False,
    )
```

```python
import functools

import jax
import jax.numpy as jnp
from jax import lax
from jax.experimental import pallas as pl
from jax.experimental.pallas import tpu as pltpu
from jax.sharding import PartitionSpec as P


def from_behind(block, axis, distance):
    devices = range(lax.axis_size(axis))
    route = [((i - distance) % len(devices), i) for i in devices]
    return lax.ppermute(block, axis, route)


def block_kernel(rows, rows_sq, land, width):
    cross = lax.dot_general(
        land, rows, (((1,), (1,)), ((), ())), preferred_element_type=jnp.float32
    )
    land_sq = jnp.sum(jnp.square(land.astype(jnp.float32)), axis=1)
    dist = rows_sq[None, :] + land_sq[:, None] - 2.0 * cross
    return jnp.exp(-width.astype(jnp.float32)[:, None] * dist).astype(jnp.bfloat16)


def class_logits(kern_t, coef):
    return lax.dot_general(
        kern_t, coef, (((0,), (0,)), ((), ())), preferred_element_type=jnp.float32
    )


def logit_gradient(logits, labels):
    top = jnp.max(logits, axis=1, keepdims=True)
    expo = jnp.exp(logits - top)
    probs = expo / jnp.sum(expo, axis=1, keepdims=True)
    classes = lax.broadcasted_iota(jnp.int32, logits.shape, 1)
    onehot = (classes == labels[:, None]).astype(jnp.float32)
    return (probs - onehot).astype(jnp.bfloat16)


def grad_terms(land, coef, width, kern_t, rows, grad_rows):
    grad_kernel = lax.dot_general(
        coef, grad_rows, (((1,), (1,)), ((), ())), preferred_element_type=jnp.float32
    )
    pull = (
        2.0 * width.astype(jnp.float32)[:, None] * grad_kernel * kern_t.astype(jnp.float32)
    ).astype(jnp.bfloat16)
    grad_coef = jnp.dot(kern_t, grad_rows, preferred_element_type=jnp.float32)
    grad_land = jnp.dot(pull, rows, preferred_element_type=jnp.float32) - jnp.sum(
        pull.astype(jnp.float32), axis=1
    )[:, None] * land.astype(jnp.float32)
    return (grad_land, grad_coef, pull)


def project_rows(pull, land):
    return lax.dot_general(pull, land, (((0,), (0,)), ((), ())), preferred_element_type=jnp.float32)


def target_block(position, step, blocks):
    return (position - step - 1) % blocks


def local(embeddings, labels, landmarks, coeffs, widths):
    rows_sq = jnp.sum(jnp.square(embeddings.astype(jnp.float32)), axis=1)
    width_d = embeddings.shape[1]
    classes = coeffs.shape[1]
    size_b = landmarks.shape[0]
    blocks = lax.axis_size("blk")
    position = lax.axis_index("blk")
    all_land, all_coef, all_width = (
        lax.all_gather(landmarks, "blk", axis=0, tiled=True),
        lax.all_gather(coeffs, "blk", axis=0, tiled=True),
        lax.all_gather(widths, "blk", axis=0, tiled=True),
    )
    kern_all = block_kernel(embeddings, rows_sq, all_land, all_width)
    partial_value = class_logits(kern_all, all_coef)
    logits = lax.psum(partial_value, "col")
    grad_rows = logit_gradient(logits, labels)
    sections = ((True, 0, size_b),)

    def pass_on(values):
        return from_behind((values[0], values[1]), "blk", 1)

    empty = tuple(
        (
            (jnp.zeros((size, width_d), jnp.float32), jnp.zeros((size, classes), jnp.float32))
            for upward, low, size in sections
        )
    )
    land_all, coef_all, pull_all = grad_terms(
        all_land, all_coef, all_width, kern_all, embeddings, grad_rows
    )
    pull_z = project_rows(pull_all, all_land)
    pull_rows = jnp.sum(pull_all.astype(jnp.float32), axis=0)

    def select(values, block, low, size):
        return lax.dynamic_slice_in_dim(values, block * size_b + low, size, 0)

    def cached_step(step, accums):
        moved = []
        for index, (upward, low, size) in enumerate(sections):
            block = target_block(position, step, blocks)
            total = (
                accums[index][0] + select(land_all, block, low, size),
                accums[index][1] + select(coef_all, block, low, size),
            )
            moved.append(pass_on(total))
        return tuple(moved)

    accums = lax.fori_loop(0, blocks - 1, cached_step, empty)
    finals = [
        (
            accums[index][0] + select(land_all, position, low, size),
            accums[index][1] + select(coef_all, position, low, size),
        )
        for index, (upward, low, size) in enumerate(sections)
    ]
    grad_landmarks = jnp.concatenate([item[0] for item in finals], axis=0)
    grad_coeffs = jnp.concatenate([item[1] for item in finals], axis=0)
    local_rows = pull_z - pull_rows[:, None] * embeddings.astype(jnp.float32)
    grad_embeddings = lax.psum_scatter(local_rows, "col", scatter_dimension=0, tiled=True)
    return (grad_landmarks, grad_coeffs, grad_embeddings)


NT = (((1,), (1,)), ((), ()))
TN = (((0,), (0,)), ((), ()))


def fused_kernel(
    classes, emb_hbm, lab_hbm, land_hbm, coef_hbm, width_hbm,
    out_land, out_coef, out_emb,
    emb, lab_ref, land_ref, coef_ref, width_ref,
    table, kern, pull, pull_t, logits, grad, acc,
    to_core, from_core, to_second, from_second, to_first, from_first, to_z, from_z,
    send_sem, z_sem, first_sem, second_sem, core_sem, back_sem, piece_sem, back_z_sem, local_sem,
):
    blk, col = lax.axis_index("blk"), lax.axis_index("col")
    size, depth = land_ref.shape
    wide = table.shape[1]
    rows = emb.shape[0]
    slab, half = 4 * size, 8 * size
    other = 1 - col
    x, y, z = blk % 2, (blk // 2) % 2, blk // 4
    my1 = x * other + y * col
    my2 = y * other + x * col
    first = (blk + (1 - 2 * my1) * (1 + col), col)
    second = (blk + (1 - 2 * my2) * (2 - col), col)
    core = (blk, other)
    far = z // 2
    toward = 1 - 2 * far
    within = z + far * (3 - 2 * z)
    nearest = [3 * far + toward * at for at in (1 - within, 2, 3)]

    def at_z(where):
        return where * 4 + blk % 4, col

    def base(c, p2, p1):
        return ((c * 2 + p2) * 2 + p1) * slab

    def piece(start, where):
        return pl.ds(pl.multiple_of(start + where * size, size), size)

    mine = emb_hbm.at[pl.ds(pl.multiple_of(col * rows, 64), rows)]
    loads = [
        pltpu.make_async_copy(src, dst, local_sem.at[n])
        for n, (src, dst) in enumerate((
            (land_hbm, land_ref), (coef_hbm, coef_ref), (width_hbm, width_ref),
            (lab_hbm, lab_ref), (mine, emb),
        ))
    ]
    for load in loads:
        load.start()

    barrier = pltpu.get_barrier_semaphore()
    peers = [first, second, core] + [at_z(where) for where in nearest]
    for peer in peers:
        pl.semaphore_signal(barrier, inc=1, device_id=peer, device_id_type=pl.DeviceIdType.MESH)

    own = piece(base(col, my2, my1), z)
    for load in loads[:3]:
        load.wait()
    eye = lax.broadcasted_iota(jnp.int32, (size, size), 0) == lax.broadcasted_iota(
        jnp.int32, (size, size), 1
    )
    width_col = jnp.sum(
        jnp.where(eye, width_ref[...].astype(jnp.float32), 0.0), axis=1, keepdims=True
    )
    tail = wide - 128
    split = tail - depth
    lanes = lax.broadcasted_iota(jnp.int32, (size, 128), 1)
    last = jnp.concatenate(
        [
            coef_ref[:, split:].astype(jnp.float32),
            jnp.zeros((size, 128 - (classes - split)), jnp.float32),
        ],
        axis=1,
    )
    last = jnp.where(lanes == classes - split, width_col, last)
    table[own, :depth] = land_ref[...]
    table[own, depth:tail] = coef_ref[:, :split]
    table[own, tail:] = last.astype(jnp.bfloat16)

    pl.semaphore_wait(barrier, len(peers))

    sends = []

    def send(src, dst, recv, device):
        copy = pltpu.make_async_remote_copy(
            src_ref=src, dst_ref=dst, send_sem=send_sem.at[len(sends)], recv_sem=recv,
            device_id=device, device_id_type=pl.DeviceIdType.MESH,
        )
        copy.start()
        sends.append(copy)

    def arrived(dst, recv):
        pltpu.make_async_remote_copy(
            src_ref=dst, dst_ref=dst, send_sem=send_sem.at[0], recv_sem=recv,
            device_id=core, device_id_type=pl.DeviceIdType.MESH,
        ).wait_recv()

    def put(where, recv, device):
        send(table.at[where], table.at[where], recv, device)

    slab_a = base(col, my2, my1)
    slab_b = base(col, my2, 1 - my1)
    slab_c = base(col, 1 - my2, my1)
    slab_d = base(col, 1 - my2, 1 - my1)
    put(own, first_sem.at[0], first)
    put(own, second_sem.at[0], second)
    for where in nearest:
        put(own, z_sem.at[z], at_z(where))
    put(own, core_sem.at[0], core)

    for load in loads[3:]:
        load.wait()
    emb_f = emb[...].astype(jnp.float32)
    eye_rows = lax.broadcasted_iota(jnp.int32, (rows, rows), 0) == lax.broadcasted_iota(
        jnp.int32, (rows, rows), 1
    )
    rows_sq = jnp.sum(jnp.square(emb_f), axis=1, keepdims=True)
    rows_sq = jnp.sum(jnp.where(eye_rows, rows_sq, 0.0), axis=0, keepdims=True)

    around = [z] + nearest

    def from_z_axis(k):
        where = piece(slab_a, around[k])
        arrived(table.at[where], z_sem.at[around[k]])
        put(where, first_sem.at[k], first)
        put(where, second_sem.at[k], second)
        put(where, core_sem.at[k], core)

    def from_first_axis(k):
        where = piece(slab_b, around[k])
        arrived(table.at[where], first_sem.at[k])
        put(where, second_sem.at[4 + k], second)
        put(where, core_sem.at[4 + k], core)

    def from_second_axis(n, k):
        where = piece((slab_c, slab_d)[n], around[k])
        arrived(table.at[where], second_sem.at[4 * n + k])
        put(where, core_sem.at[8 + 4 * n + k], core)

    def widths_of(where):
        end = table[where, tail:].astype(jnp.float32)
        at = lax.broadcasted_iota(jnp.int32, end.shape, 1) == classes - split
        return jnp.sum(jnp.where(at, end, 0.0), axis=1, keepdims=True)

    def forward(start, fresh):
        where = pl.ds(pl.multiple_of(start, half), half)
        land = table[where, :depth]
        cross = lax.dot_general(land, emb[...], NT, preferred_element_type=jnp.float32)
        land_sq = jnp.sum(jnp.square(land.astype(jnp.float32)), axis=1, keepdims=True)
        dist = (rows_sq + land_sq) - 2.0 * cross
        value = jnp.exp(-widths_of(where) * dist).astype(jnp.bfloat16)
        kern[where, :] = value
        part = lax.dot_general(
            value, table[where, depth:], TN, preferred_element_type=jnp.float32
        )
        if fresh:
            logits[...] = part
        else:
            logits[...] += part

    from_first_axis(0)
    from_second_axis(0, 0)
    from_z_axis(1)
    from_second_axis(1, 0)
    from_first_axis(1)
    from_second_axis(0, 1)
    from_z_axis(2)
    from_first_axis(2)
    from_second_axis(1, 1)
    from_z_axis(3)
    from_second_axis(0, 2)
    from_first_axis(3)
    from_second_axis(1, 2)
    forward(base(col, my2, 0), True)
    from_second_axis(0, 3)
    for n, start in enumerate((base(other, my1, my2), base(other, my1, 1 - my2))):
        for k in range(4):
            arrived(table.at[piece(start, around[k])], core_sem.at[4 * n + k])
    forward(base(other, my1, 0), False)
    from_second_axis(1, 3)
    forward(base(col, 1 - my2, 0), False)
    for n, start in enumerate((base(other, 1 - my1, my2), base(other, 1 - my1, 1 - my2))):
        for k in range(4):
            arrived(table.at[piece(start, around[k])], core_sem.at[8 + 4 * n + k])
    forward(base(other, 1 - my1, 0), False)

    all_rows = lab_ref.shape[0]
    mine = lax.broadcasted_iota(jnp.int32, (rows, all_rows), 1) == (
        lax.broadcasted_iota(jnp.int32, (rows, all_rows), 0) + col * rows
    )
    label = jnp.sum(
        jnp.where(mine, lab_ref[...].astype(jnp.float32)[None, :], 0.0), axis=1, keepdims=True
    ).astype(jnp.int32)
    place = lax.broadcasted_iota(jnp.int32, logits.shape, 1)
    value = jnp.where(place < classes, logits[...], -jnp.inf)
    expo = jnp.exp(value - jnp.max(value, axis=1, keepdims=True))
    probs = expo / jnp.sum(expo, axis=1, keepdims=True)
    grad[...] = (probs - jnp.where(place == label, 1.0, 0.0)).astype(jnp.bfloat16)

    def terms(start):
        where = pl.ds(pl.multiple_of(start, half), half)
        grad_kernel = lax.dot_general(
            table[where, depth:], grad[...], NT, preferred_element_type=jnp.float32
        )
        tug = (
            2.0 * widths_of(where) * grad_kernel * kern[where, :].astype(jnp.float32)
        ).astype(jnp.bfloat16)
        pull[where, :] = tug
        land = jnp.dot(tug, emb[...], preferred_element_type=jnp.float32)
        land -= jnp.sum(tug.astype(jnp.float32), axis=1, keepdims=True) * table[
            where, :depth
        ].astype(jnp.float32)
        coef = jnp.dot(kern[where, :], grad[...], preferred_element_type=jnp.float32)
        return land, coef

    def part(index):
        return pl.ds(pl.multiple_of(index * slab, slab), slab)

    def for_core(n, p2):
        land, coef = terms(base(other, p2, 0))
        to_core[n, :, :depth] = land.astype(jnp.bfloat16)
        to_core[n, :, depth:] = coef.astype(jnp.bfloat16)
        for m, p1 in enumerate((1 - my2, my2)):
            send(
                to_core.at[n, part(p1)], from_core.at[n, part(p1)],
                back_sem.at[2 * n + m], core,
            )

    def for_self(n, p2):
        land, coef = terms(base(col, p2, 0))
        acc[n, :, :depth] = land
        acc[n, :, depth:] = coef

    def target(p1, where):
        start = p1 * slab + where * size
        return pl.ds(pl.multiple_of(start, size), size)

    order = around[::-1]
    for_core(0, 1 - my1)
    for_self(0, 1 - my2)
    for m, p1 in enumerate((1 - my1, my1)):
        arrived(from_core.at[0, part(p1)], back_sem.at[m])
    for n in range(4):
        for m, p1 in enumerate((1 - my1, my1)):
            where = target(p1, order[n])
            total = acc[0, where, :] + from_core[0, where, :].astype(jnp.float32)
            to_second[n, m] = total.astype(jnp.bfloat16)
            send(to_second.at[n, m], from_second.at[n, m], piece_sem.at[n, m], second)
    for_core(1, my1)
    for_self(1, my2)
    for m, p1 in enumerate((1 - my1, my1)):
        arrived(from_core.at[1, part(p1)], back_sem.at[2 + m])

    def summed(n, m, p1, k):
        where = target(p1, k)
        arrived(from_second.at[n, m], piece_sem.at[n, m])
        return (
            acc[1, where, :]
            + from_core[1, where, :].astype(jnp.float32)
            + from_second[n, m].astype(jnp.float32)
        )

    def pass_first(n):
        to_first[n] = summed(n, 0, 1 - my1, order[n]).astype(jnp.bfloat16)
        send(to_first.at[n], from_first.at[n], piece_sem.at[n, 2], first)

    def collect(n):
        total = summed(n, 1, my1, order[n])
        arrived(from_first.at[n], piece_sem.at[n, 2])
        return total + from_first[n].astype(jnp.float32)

    def pass_z(n):
        to_z[n] = collect(n).astype(jnp.bfloat16)
        send(to_z.at[n], from_z.at[z], back_z_sem.at[z], at_z(order[n]))

    def project(n):
        where = pl.ds(n * slab, slab)
        tug = pull_t[where, :]
        drawn = jnp.dot(tug, table[:, :depth], preferred_element_type=jnp.float32)
        out_emb[where, :] = drawn - jnp.sum(
            tug.astype(jnp.float32), axis=1, keepdims=True
        ) * emb[where, :].astype(jnp.float32)

    pull_t[...] = pull[...].T
    pass_first(0)
    project(0)
    pass_first(1)
    pass_z(0)
    project(1)
    pass_first(2)
    pass_z(1)
    project(2)
    pass_first(3)
    pass_z(2)
    result = collect(3)
    for where in order[:3]:
        arrived(from_z.at[where], back_z_sem.at[where])
        result += from_z[where].astype(jnp.float32)
    out_land[...] = result[:, :depth]
    out_coef[...] = result[:, depth : depth + classes]

    for copy in sends:
        copy.wait_send()


def place_kernel(emb, coef, land, out_emb, out_coef, out_land, sem):
    stores = [
        pltpu.make_async_copy(src, dst, sem.at[n])
        for n, (src, dst) in enumerate(((emb, out_emb), (coef, out_coef), (land, out_land)))
    ]
    for store in stores:
        store.start()
    for store in stores:
        store.wait()


def fused(embeddings, labels, landmarks, coeffs, widths):
    size, depth = landmarks.shape
    classes = coeffs.shape[1]
    rows = embeddings.shape[0] // 2
    padded = (classes // 128 + 1) * 128
    wide = depth + padded
    count, half = 32 * size, 8 * size
    vmem = pl.BlockSpec(memory_space=pltpu.VMEM)
    hbm = pl.BlockSpec(memory_space=pltpu.HBM)
    anywhere = pl.BlockSpec(memory_space=pl.ANY)
    bf16, f32 = jnp.bfloat16, jnp.float32
    out_shape = (
        jax.ShapeDtypeStruct((size, depth), f32),
        jax.ShapeDtypeStruct((size, classes), f32),
        jax.ShapeDtypeStruct((rows, depth), f32),
    )
    results = pl.pallas_call(
        functools.partial(fused_kernel, classes),
        out_shape=tuple(pltpu.VMEM(out.shape, out.dtype) for out in out_shape),
        in_specs=[hbm] * 5,
        out_specs=(vmem,) * 3,
        scratch_shapes=[
            pltpu.VMEM((rows, depth), bf16),
            pltpu.VMEM(labels.shape, labels.dtype),
            pltpu.VMEM(landmarks.shape, bf16),
            pltpu.VMEM(coeffs.shape, bf16),
            pltpu.VMEM((1, size), bf16),
            pltpu.VMEM((count, wide), bf16),
            pltpu.VMEM((count, rows), bf16),
            pltpu.VMEM((count, rows), bf16),
            pltpu.VMEM((rows, count), bf16),
            pltpu.VMEM((rows, padded), f32),
            pltpu.VMEM((rows, padded), bf16),
            pltpu.VMEM((2, half, wide), f32),
            pltpu.VMEM((2, half, wide), bf16),
            pltpu.VMEM((2, half, wide), bf16),
            pltpu.VMEM((4, 2, size, wide), bf16),
            pltpu.VMEM((4, 2, size, wide), bf16),
            pltpu.VMEM((4, size, wide), bf16),
            pltpu.VMEM((4, size, wide), bf16),
            pltpu.VMEM((3, size, wide), bf16),
            pltpu.VMEM((4, size, wide), bf16),
            pltpu.SemaphoreType.DMA((50,)),
            pltpu.SemaphoreType.DMA((4,)),
            pltpu.SemaphoreType.DMA((4,)),
            pltpu.SemaphoreType.DMA((8,)),
            pltpu.SemaphoreType.DMA((16,)),
            pltpu.SemaphoreType.DMA((4,)),
            pltpu.SemaphoreType.DMA((4, 3)),
            pltpu.SemaphoreType.DMA((4,)),
            pltpu.SemaphoreType.DMA((5,)),
        ],
        compiler_params=pltpu.CompilerParams(
            collective_id=0, has_side_effects=True, vmem_limit_bytes=60 * 2**20
        ),
    )(embeddings, labels, landmarks, coeffs, widths[None, :])
    grad_emb, grad_coef, grad_land = pl.pallas_call(
        place_kernel,
        out_shape=out_shape[::-1],
        in_specs=[vmem] * 3,
        out_specs=(anywhere,) * 3,
        scratch_shapes=[pltpu.SemaphoreType.DMA((3,))],
        compiler_params=pltpu.CompilerParams(vmem_limit_bytes=16 * 2**20),
    )(*results[::-1])
    return grad_land, grad_coef, grad_emb


def fits_fused(mesh):
    return mesh.shape["blk"] == 16 and mesh.shape["col"] == 2


def solution(mesh):
    return jax.shard_map(
        fused if fits_fused(mesh) else local,
        mesh=mesh,
        in_specs=(
            P("blk", None),
            P("blk"),
            P(("blk", "col"), None),
            P(("blk", "col"), None),
            P(("blk", "col")),
        ),
        out_specs=(P(("blk", "col"), None), P(("blk", "col"), None), P(("blk", "col"), None)),
        check_vma=False,
    )
```

```python
import functools

import jax
import jax.numpy as jnp
from jax import lax
from jax.experimental import pallas as pl
from jax.experimental.pallas import tpu as pltpu
from jax.sharding import PartitionSpec as P


def from_behind(block, axis, distance):
    devices = range(lax.axis_size(axis))
    route = [((i - distance) % len(devices), i) for i in devices]
    return lax.ppermute(block, axis, route)


def block_kernel(rows, rows_sq, land, width):
    cross = lax.dot_general(
        land, rows, (((1,), (1,)), ((), ())), preferred_element_type=jnp.float32
    )
    land_sq = jnp.sum(jnp.square(land.astype(jnp.float32)), axis=1)
    dist = rows_sq[None, :] + land_sq[:, None] - 2.0 * cross
    return jnp.exp(-width.astype(jnp.float32)[:, None] * dist).astype(jnp.bfloat16)


def class_logits(kern_t, coef):
    return lax.dot_general(
        kern_t, coef, (((0,), (0,)), ((), ())), preferred_element_type=jnp.float32
    )


def logit_gradient(logits, labels):
    top = jnp.max(logits, axis=1, keepdims=True)
    expo = jnp.exp(logits - top)
    probs = expo / jnp.sum(expo, axis=1, keepdims=True)
    classes = lax.broadcasted_iota(jnp.int32, logits.shape, 1)
    onehot = (classes == labels[:, None]).astype(jnp.float32)
    return (probs - onehot).astype(jnp.bfloat16)


def grad_terms(land, coef, width, kern_t, rows, grad_rows):
    grad_kernel = lax.dot_general(
        coef, grad_rows, (((1,), (1,)), ((), ())), preferred_element_type=jnp.float32
    )
    pull = (
        2.0 * width.astype(jnp.float32)[:, None] * grad_kernel * kern_t.astype(jnp.float32)
    ).astype(jnp.bfloat16)
    grad_coef = jnp.dot(kern_t, grad_rows, preferred_element_type=jnp.float32)
    grad_land = jnp.dot(pull, rows, preferred_element_type=jnp.float32) - jnp.sum(
        pull.astype(jnp.float32), axis=1
    )[:, None] * land.astype(jnp.float32)
    return (grad_land, grad_coef, pull)


def project_rows(pull, land):
    return lax.dot_general(pull, land, (((0,), (0,)), ((), ())), preferred_element_type=jnp.float32)


def target_block(position, step, blocks):
    return (position - step - 1) % blocks


def local(embeddings, labels, landmarks, coeffs, widths):
    rows_sq = jnp.sum(jnp.square(embeddings.astype(jnp.float32)), axis=1)
    width_d = embeddings.shape[1]
    classes = coeffs.shape[1]
    size_b = landmarks.shape[0]
    blocks = lax.axis_size("blk")
    position = lax.axis_index("blk")
    all_land, all_coef, all_width = (
        lax.all_gather(landmarks, "blk", axis=0, tiled=True),
        lax.all_gather(coeffs, "blk", axis=0, tiled=True),
        lax.all_gather(widths, "blk", axis=0, tiled=True),
    )
    kern_all = block_kernel(embeddings, rows_sq, all_land, all_width)
    partial_value = class_logits(kern_all, all_coef)
    logits = lax.psum(partial_value, "col")
    grad_rows = logit_gradient(logits, labels)
    sections = ((True, 0, size_b),)

    def pass_on(values):
        return from_behind((values[0], values[1]), "blk", 1)

    empty = tuple(
        (
            (jnp.zeros((size, width_d), jnp.float32), jnp.zeros((size, classes), jnp.float32))
            for upward, low, size in sections
        )
    )
    land_all, coef_all, pull_all = grad_terms(
        all_land, all_coef, all_width, kern_all, embeddings, grad_rows
    )
    pull_z = project_rows(pull_all, all_land)
    pull_rows = jnp.sum(pull_all.astype(jnp.float32), axis=0)

    def select(values, block, low, size):
        return lax.dynamic_slice_in_dim(values, block * size_b + low, size, 0)

    def cached_step(step, accums):
        moved = []
        for index, (upward, low, size) in enumerate(sections):
            block = target_block(position, step, blocks)
            total = (
                accums[index][0] + select(land_all, block, low, size),
                accums[index][1] + select(coef_all, block, low, size),
            )
            moved.append(pass_on(total))
        return tuple(moved)

    accums = lax.fori_loop(0, blocks - 1, cached_step, empty)
    finals = [
        (
            accums[index][0] + select(land_all, position, low, size),
            accums[index][1] + select(coef_all, position, low, size),
        )
        for index, (upward, low, size) in enumerate(sections)
    ]
    grad_landmarks = jnp.concatenate([item[0] for item in finals], axis=0)
    grad_coeffs = jnp.concatenate([item[1] for item in finals], axis=0)
    local_rows = pull_z - pull_rows[:, None] * embeddings.astype(jnp.float32)
    grad_embeddings = lax.psum_scatter(local_rows, "col", scatter_dimension=0, tiled=True)
    return (grad_landmarks, grad_coeffs, grad_embeddings)


NT = (((1,), (1,)), ((), ()))
TN = (((0,), (0,)), ((), ()))


def fused_kernel(
    classes, emb_hbm, lab_hbm, land_hbm, coef_hbm, width_hbm,
    out_land, out_coef, out_emb,
    emb, lab_ref, land_ref, coef_ref, width_ref,
    table, kern, pull, pull_t, logits, grad, acc,
    to_core, from_core, to_second, from_second, to_first, from_first, to_z, from_z,
    send_sem, z_sem, first_sem, second_sem, core_sem, back_sem, piece_sem, back_z_sem, local_sem,
):
    blk, col = lax.axis_index("blk"), lax.axis_index("col")
    size, depth = land_ref.shape
    wide = table.shape[1]
    rows = emb.shape[0]
    slab, half = 4 * size, 8 * size
    other = 1 - col
    x, y, z = blk % 2, (blk // 2) % 2, blk // 4
    my1 = x * other + y * col
    my2 = y * other + x * col
    first = (blk + (1 - 2 * my1) * (1 + col), col)
    second = (blk + (1 - 2 * my2) * (2 - col), col)
    core = (blk, other)
    far = z // 2
    toward = 1 - 2 * far
    within = z + far * (3 - 2 * z)
    nearest = [3 * far + toward * at for at in (1 - within, 2, 3)]

    def at_z(where):
        return where * 4 + blk % 4, col

    def base(c, p2, p1):
        return ((c * 2 + p2) * 2 + p1) * slab

    def piece(start, where):
        return pl.ds(pl.multiple_of(start + where * size, size), size)

    mine = emb_hbm.at[pl.ds(pl.multiple_of(col * rows, 64), rows)]
    loads = [
        pltpu.make_async_copy(src, dst, local_sem.at[n])
        for n, (src, dst) in enumerate((
            (land_hbm, land_ref), (coef_hbm, coef_ref), (width_hbm, width_ref),
            (lab_hbm, lab_ref), (mine, emb),
        ))
    ]
    for load in loads:
        load.start()

    barrier = pltpu.get_barrier_semaphore()
    peers = [first, second, core] + [at_z(where) for where in nearest]
    for peer in peers:
        pl.semaphore_signal(barrier, inc=1, device_id=peer, device_id_type=pl.DeviceIdType.MESH)

    own = piece(base(col, my2, my1), z)
    for load in loads[:3]:
        load.wait()
    eye = lax.broadcasted_iota(jnp.int32, (size, size), 0) == lax.broadcasted_iota(
        jnp.int32, (size, size), 1
    )
    width_col = jnp.sum(
        jnp.where(eye, width_ref[...].astype(jnp.float32), 0.0), axis=1, keepdims=True
    )
    tail = wide - 128
    split = tail - depth
    lanes = lax.broadcasted_iota(jnp.int32, (size, 128), 1)
    last = jnp.concatenate(
        [
            coef_ref[:, split:].astype(jnp.float32),
            jnp.zeros((size, 128 - (classes - split)), jnp.float32),
        ],
        axis=1,
    )
    last = jnp.where(lanes == classes - split, width_col, last)
    table[own, :depth] = land_ref[...]
    table[own, depth:tail] = coef_ref[:, :split]
    table[own, tail:] = last.astype(jnp.bfloat16)

    pl.semaphore_wait(barrier, len(peers))

    sends = []

    def send(src, dst, recv, device):
        copy = pltpu.make_async_remote_copy(
            src_ref=src, dst_ref=dst, send_sem=send_sem.at[len(sends)], recv_sem=recv,
            device_id=device, device_id_type=pl.DeviceIdType.MESH,
        )
        copy.start()
        sends.append(copy)

    def arrived(dst, recv):
        pltpu.make_async_remote_copy(
            src_ref=dst, dst_ref=dst, send_sem=send_sem.at[0], recv_sem=recv,
            device_id=core, device_id_type=pl.DeviceIdType.MESH,
        ).wait_recv()

    def put(where, recv, device):
        send(table.at[where], table.at[where], recv, device)

    slab_a = base(col, my2, my1)
    slab_b = base(col, my2, 1 - my1)
    slab_c = base(col, 1 - my2, my1)
    slab_d = base(col, 1 - my2, 1 - my1)
    for where in nearest:
        put(own, z_sem.at[z], at_z(where))
    put(own, second_sem.at[0], second)
    put(own, first_sem.at[0], first)
    put(own, core_sem.at[0], core)

    for load in loads[3:]:
        load.wait()
    emb_f = emb[...].astype(jnp.float32)
    eye_rows = lax.broadcasted_iota(jnp.int32, (rows, rows), 0) == lax.broadcasted_iota(
        jnp.int32, (rows, rows), 1
    )
    rows_sq = jnp.sum(jnp.square(emb_f), axis=1, keepdims=True)
    rows_sq = jnp.sum(jnp.where(eye_rows, rows_sq, 0.0), axis=0, keepdims=True)

    around = [z] + nearest

    def from_z_axis(k):
        where = piece(slab_a, around[k])
        arrived(table.at[where], z_sem.at[around[k]])
        put(where, first_sem.at[k], first)
        put(where, second_sem.at[k], second)
        put(where, core_sem.at[k], core)

    def from_first_axis(k):
        where = piece(slab_b, around[k])
        arrived(table.at[where], first_sem.at[k])
        put(where, second_sem.at[4 + k], second)
        put(where, core_sem.at[4 + k], core)

    def from_second_axis(n, k):
        where = piece((slab_c, slab_d)[n], around[k])
        arrived(table.at[where], second_sem.at[4 * n + k])
        put(where, core_sem.at[8 + 4 * n + k], core)

    def widths_of(where):
        end = table[where, tail:].astype(jnp.float32)
        at = lax.broadcasted_iota(jnp.int32, end.shape, 1) == classes - split
        return jnp.sum(jnp.where(at, end, 0.0), axis=1, keepdims=True)

    def forward(start, fresh):
        where = pl.ds(pl.multiple_of(start, half), half)
        land = table[where, :depth]
        cross = lax.dot_general(land, emb[...], NT, preferred_element_type=jnp.float32)
        land_sq = jnp.sum(jnp.square(land.astype(jnp.float32)), axis=1, keepdims=True)
        dist = (rows_sq + land_sq) - 2.0 * cross
        value = jnp.exp(-widths_of(where) * dist).astype(jnp.bfloat16)
        kern[where, :] = value
        part = lax.dot_general(
            value, table[where, depth:], TN, preferred_element_type=jnp.float32
        )
        if fresh:
            logits[...] = part
        else:
            logits[...] += part

    for k in (1, 2, 3):
        from_z_axis(k)
    for k in range(4):
        from_first_axis(k)
    forward(base(col, my2, 0), True)
    for k in range(4):
        from_second_axis(0, k)
    for n, start in enumerate((base(other, my1, my2), base(other, my1, 1 - my2))):
        for k in range(4):
            arrived(table.at[piece(start, around[k])], core_sem.at[4 * n + k])
    forward(base(other, my1, 0), False)
    for k in range(4):
        from_second_axis(1, k)
    forward(base(col, 1 - my2, 0), False)
    for n, start in enumerate((base(other, 1 - my1, my2), base(other, 1 - my1, 1 - my2))):
        for k in range(4):
            arrived(table.at[piece(start, around[k])], core_sem.at[8 + 4 * n + k])
    forward(base(other, 1 - my1, 0), False)

    all_rows = lab_ref.shape[0]
    mine = lax.broadcasted_iota(jnp.int32, (rows, all_rows), 1) == (
        lax.broadcasted_iota(jnp.int32, (rows, all_rows), 0) + col * rows
    )
    label = jnp.sum(
        jnp.where(mine, lab_ref[...].astype(jnp.float32)[None, :], 0.0), axis=1, keepdims=True
    ).astype(jnp.int32)
    place = lax.broadcasted_iota(jnp.int32, logits.shape, 1)
    value = jnp.where(place < classes, logits[...], -jnp.inf)
    expo = jnp.exp(value - jnp.max(value, axis=1, keepdims=True))
    probs = expo / jnp.sum(expo, axis=1, keepdims=True)
    grad[...] = (probs - jnp.where(place == label, 1.0, 0.0)).astype(jnp.bfloat16)

    def terms(start):
        where = pl.ds(pl.multiple_of(start, half), half)
        grad_kernel = lax.dot_general(
            table[where, depth:], grad[...], NT, preferred_element_type=jnp.float32
        )
        tug = (
            2.0 * widths_of(where) * grad_kernel * kern[where, :].astype(jnp.float32)
        ).astype(jnp.bfloat16)
        pull[where, :] = tug
        land = jnp.dot(tug, emb[...], preferred_element_type=jnp.float32)
        land -= jnp.sum(tug.astype(jnp.float32), axis=1, keepdims=True) * table[
            where, :depth
        ].astype(jnp.float32)
        coef = jnp.dot(kern[where, :], grad[...], preferred_element_type=jnp.float32)
        return land, coef

    def part(index):
        return pl.ds(pl.multiple_of(index * slab, slab), slab)

    def for_core(n, p2):
        land, coef = terms(base(other, p2, 0))
        to_core[n, :, :depth] = land.astype(jnp.bfloat16)
        to_core[n, :, depth:] = coef.astype(jnp.bfloat16)
        for m, p1 in enumerate((1 - my2, my2)):
            send(
                to_core.at[n, part(p1)], from_core.at[n, part(p1)],
                back_sem.at[2 * n + m], core,
            )

    def for_self(n, p2):
        land, coef = terms(base(col, p2, 0))
        acc[n, :, :depth] = land
        acc[n, :, depth:] = coef

    def target(p1, where):
        start = p1 * slab + where * size
        return pl.ds(pl.multiple_of(start, size), size)

    order = around[::-1]
    for_core(0, 1 - my1)
    for_self(0, 1 - my2)
    for m, p1 in enumerate((1 - my1, my1)):
        arrived(from_core.at[0, part(p1)], back_sem.at[m])
    for n in range(4):
        for m, p1 in enumerate((1 - my1, my1)):
            where = target(p1, order[n])
            total = acc[0, where, :] + from_core[0, where, :].astype(jnp.float32)
            to_second[n, m] = total.astype(jnp.bfloat16)
            send(to_second.at[n, m], from_second.at[n, m], piece_sem.at[n, m], second)
    for_core(1, my1)
    for_self(1, my2)
    for m, p1 in enumerate((1 - my1, my1)):
        arrived(from_core.at[1, part(p1)], back_sem.at[2 + m])

    def summed(n, m, p1, k):
        where = target(p1, k)
        arrived(from_second.at[n, m], piece_sem.at[n, m])
        return (
            acc[1, where, :]
            + from_core[1, where, :].astype(jnp.float32)
            + from_second[n, m].astype(jnp.float32)
        )

    def pass_first(n):
        to_first[n] = summed(n, 0, 1 - my1, order[n]).astype(jnp.bfloat16)
        send(to_first.at[n], from_first.at[n], piece_sem.at[n, 2], first)

    def collect(n):
        total = summed(n, 1, my1, order[n])
        arrived(from_first.at[n], piece_sem.at[n, 2])
        return total + from_first[n].astype(jnp.float32)

    def pass_z(n):
        to_z[n] = collect(n).astype(jnp.bfloat16)
        send(to_z.at[n], from_z.at[z], back_z_sem.at[z], at_z(order[n]))

    def project(n):
        where = pl.ds(n * slab, slab)
        tug = pull_t[where, :]
        drawn = jnp.dot(tug, table[:, :depth], preferred_element_type=jnp.float32)
        out_emb[where, :] = drawn - jnp.sum(
            tug.astype(jnp.float32), axis=1, keepdims=True
        ) * emb[where, :].astype(jnp.float32)

    pull_t[...] = pull[...].T
    pass_first(0)
    project(0)
    pass_first(1)
    pass_z(0)
    project(1)
    pass_first(2)
    pass_z(1)
    project(2)
    pass_first(3)
    pass_z(2)
    result = collect(3)
    for where in order[:3]:
        arrived(from_z.at[where], back_z_sem.at[where])
        result += from_z[where].astype(jnp.float32)
    out_land[...] = result[:, :depth]
    out_coef[...] = result[:, depth : depth + classes]

    for copy in sends:
        copy.wait_send()


def place_kernel(emb, coef, land, out_emb, out_coef, out_land, sem):
    stores = [
        pltpu.make_async_copy(src, dst, sem.at[n])
        for n, (src, dst) in enumerate(((emb, out_emb), (coef, out_coef), (land, out_land)))
    ]
    for store in stores:
        store.start()
    for store in stores:
        store.wait()


def fused(embeddings, labels, landmarks, coeffs, widths):
    size, depth = landmarks.shape
    classes = coeffs.shape[1]
    rows = embeddings.shape[0] // 2
    padded = (classes // 128 + 1) * 128
    wide = depth + padded
    count, half = 32 * size, 8 * size
    vmem = pl.BlockSpec(memory_space=pltpu.VMEM)
    hbm = pl.BlockSpec(memory_space=pltpu.HBM)
    anywhere = pl.BlockSpec(memory_space=pl.ANY)
    bf16, f32 = jnp.bfloat16, jnp.float32
    out_shape = (
        jax.ShapeDtypeStruct((size, depth), f32),
        jax.ShapeDtypeStruct((size, classes), f32),
        jax.ShapeDtypeStruct((rows, depth), f32),
    )
    results = pl.pallas_call(
        functools.partial(fused_kernel, classes),
        out_shape=tuple(pltpu.VMEM(out.shape, out.dtype) for out in out_shape),
        in_specs=[hbm] * 5,
        out_specs=(vmem,) * 3,
        scratch_shapes=[
            pltpu.VMEM((rows, depth), bf16),
            pltpu.VMEM(labels.shape, labels.dtype),
            pltpu.VMEM(landmarks.shape, bf16),
            pltpu.VMEM(coeffs.shape, bf16),
            pltpu.VMEM((1, size), bf16),
            pltpu.VMEM((count, wide), bf16),
            pltpu.VMEM((count, rows), bf16),
            pltpu.VMEM((count, rows), bf16),
            pltpu.VMEM((rows, count), bf16),
            pltpu.VMEM((rows, padded), f32),
            pltpu.VMEM((rows, padded), bf16),
            pltpu.VMEM((2, half, wide), f32),
            pltpu.VMEM((2, half, wide), bf16),
            pltpu.VMEM((2, half, wide), bf16),
            pltpu.VMEM((4, 2, size, wide), bf16),
            pltpu.VMEM((4, 2, size, wide), bf16),
            pltpu.VMEM((4, size, wide), bf16),
            pltpu.VMEM((4, size, wide), bf16),
            pltpu.VMEM((3, size, wide), bf16),
            pltpu.VMEM((4, size, wide), bf16),
            pltpu.SemaphoreType.DMA((50,)),
            pltpu.SemaphoreType.DMA((4,)),
            pltpu.SemaphoreType.DMA((4,)),
            pltpu.SemaphoreType.DMA((8,)),
            pltpu.SemaphoreType.DMA((16,)),
            pltpu.SemaphoreType.DMA((4,)),
            pltpu.SemaphoreType.DMA((4, 3)),
            pltpu.SemaphoreType.DMA((4,)),
            pltpu.SemaphoreType.DMA((5,)),
        ],
        compiler_params=pltpu.CompilerParams(
            collective_id=0, has_side_effects=True, vmem_limit_bytes=60 * 2**20
        ),
    )(embeddings, labels, landmarks, coeffs, widths[None, :])
    grad_emb, grad_coef, grad_land = pl.pallas_call(
        place_kernel,
        out_shape=out_shape[::-1],
        in_specs=[vmem] * 3,
        out_specs=(anywhere,) * 3,
        scratch_shapes=[pltpu.SemaphoreType.DMA((3,))],
        compiler_params=pltpu.CompilerParams(vmem_limit_bytes=16 * 2**20),
    )(*results[::-1])
    return grad_land, grad_coef, grad_emb


def fits_fused(mesh):
    return mesh.shape["blk"] == 16 and mesh.shape["col"] == 2


def solution(mesh):
    return jax.shard_map(
        fused if fits_fused(mesh) else local,
        mesh=mesh,
        in_specs=(
            P("blk", None),
            P("blk"),
            P(("blk", "col"), None),
            P(("blk", "col"), None),
            P(("blk", "col")),
        ),
        out_specs=(P(("blk", "col"), None), P(("blk", "col"), None), P(("blk", "col"), None)),
        check_vma=False,
    )
```

```python
import functools

import jax
import jax.numpy as jnp
from jax import lax
from jax.experimental import pallas as pl
from jax.experimental.pallas import tpu as pltpu
from jax.sharding import PartitionSpec as P


def from_behind(block, axis, distance):
    devices = range(lax.axis_size(axis))
    route = [((i - distance) % len(devices), i) for i in devices]
    return lax.ppermute(block, axis, route)


def block_kernel(rows, rows_sq, land, width):
    cross = lax.dot_general(
        land, rows, (((1,), (1,)), ((), ())), preferred_element_type=jnp.float32
    )
    land_sq = jnp.sum(jnp.square(land.astype(jnp.float32)), axis=1)
    dist = rows_sq[None, :] + land_sq[:, None] - 2.0 * cross
    return jnp.exp(-width.astype(jnp.float32)[:, None] * dist).astype(jnp.bfloat16)


def class_logits(kern_t, coef):
    return lax.dot_general(
        kern_t, coef, (((0,), (0,)), ((), ())), preferred_element_type=jnp.float32
    )


def logit_gradient(logits, labels):
    top = jnp.max(logits, axis=1, keepdims=True)
    expo = jnp.exp(logits - top)
    probs = expo / jnp.sum(expo, axis=1, keepdims=True)
    classes = lax.broadcasted_iota(jnp.int32, logits.shape, 1)
    onehot = (classes == labels[:, None]).astype(jnp.float32)
    return (probs - onehot).astype(jnp.bfloat16)


def grad_terms(land, coef, width, kern_t, rows, grad_rows):
    grad_kernel = lax.dot_general(
        coef, grad_rows, (((1,), (1,)), ((), ())), preferred_element_type=jnp.float32
    )
    pull = (
        2.0 * width.astype(jnp.float32)[:, None] * grad_kernel * kern_t.astype(jnp.float32)
    ).astype(jnp.bfloat16)
    grad_coef = jnp.dot(kern_t, grad_rows, preferred_element_type=jnp.float32)
    grad_land = jnp.dot(pull, rows, preferred_element_type=jnp.float32) - jnp.sum(
        pull.astype(jnp.float32), axis=1
    )[:, None] * land.astype(jnp.float32)
    return (grad_land, grad_coef, pull)


def project_rows(pull, land):
    return lax.dot_general(pull, land, (((0,), (0,)), ((), ())), preferred_element_type=jnp.float32)


def target_block(position, step, blocks):
    return (position - step - 1) % blocks


def local(embeddings, labels, landmarks, coeffs, widths):
    rows_sq = jnp.sum(jnp.square(embeddings.astype(jnp.float32)), axis=1)
    width_d = embeddings.shape[1]
    classes = coeffs.shape[1]
    size_b = landmarks.shape[0]
    blocks = lax.axis_size("blk")
    position = lax.axis_index("blk")
    all_land, all_coef, all_width = (
        lax.all_gather(landmarks, "blk", axis=0, tiled=True),
        lax.all_gather(coeffs, "blk", axis=0, tiled=True),
        lax.all_gather(widths, "blk", axis=0, tiled=True),
    )
    kern_all = block_kernel(embeddings, rows_sq, all_land, all_width)
    partial_value = class_logits(kern_all, all_coef)
    logits = lax.psum(partial_value, "col")
    grad_rows = logit_gradient(logits, labels)
    sections = ((True, 0, size_b),)

    def pass_on(values):
        return from_behind((values[0], values[1]), "blk", 1)

    empty = tuple(
        (
            (jnp.zeros((size, width_d), jnp.float32), jnp.zeros((size, classes), jnp.float32))
            for upward, low, size in sections
        )
    )
    land_all, coef_all, pull_all = grad_terms(
        all_land, all_coef, all_width, kern_all, embeddings, grad_rows
    )
    pull_z = project_rows(pull_all, all_land)
    pull_rows = jnp.sum(pull_all.astype(jnp.float32), axis=0)

    def select(values, block, low, size):
        return lax.dynamic_slice_in_dim(values, block * size_b + low, size, 0)

    def cached_step(step, accums):
        moved = []
        for index, (upward, low, size) in enumerate(sections):
            block = target_block(position, step, blocks)
            total = (
                accums[index][0] + select(land_all, block, low, size),
                accums[index][1] + select(coef_all, block, low, size),
            )
            moved.append(pass_on(total))
        return tuple(moved)

    accums = lax.fori_loop(0, blocks - 1, cached_step, empty)
    finals = [
        (
            accums[index][0] + select(land_all, position, low, size),
            accums[index][1] + select(coef_all, position, low, size),
        )
        for index, (upward, low, size) in enumerate(sections)
    ]
    grad_landmarks = jnp.concatenate([item[0] for item in finals], axis=0)
    grad_coeffs = jnp.concatenate([item[1] for item in finals], axis=0)
    local_rows = pull_z - pull_rows[:, None] * embeddings.astype(jnp.float32)
    grad_embeddings = lax.psum_scatter(local_rows, "col", scatter_dimension=0, tiled=True)
    return (grad_landmarks, grad_coeffs, grad_embeddings)


NT = (((1,), (1,)), ((), ()))
TN = (((0,), (0,)), ((), ()))


def fused_kernel(
    classes, emb_hbm, lab_hbm, land_hbm, coef_hbm, width_hbm,
    out_land, out_coef, out_emb,
    emb, lab_ref, land_ref, coef_ref, width_ref,
    table, kern, pull, pull_t, logits, grad, acc,
    to_core, from_core, to_second, from_second, to_first, from_first, to_z, from_z,
    send_sem, z_sem, first_sem, second_sem, core_sem, back_sem, piece_sem, back_z_sem, local_sem,
):
    blk, col = lax.axis_index("blk"), lax.axis_index("col")
    size, depth = land_ref.shape
    wide = table.shape[1]
    rows = emb.shape[0]
    slab, half = 4 * size, 8 * size
    other = 1 - col
    x, y, z = blk % 2, (blk // 2) % 2, blk // 4
    my1 = x * other + y * col
    my2 = y * other + x * col
    first = (blk + (1 - 2 * my1) * (1 + col), col)
    second = (blk + (1 - 2 * my2) * (2 - col), col)
    core = (blk, other)
    far = z // 2
    toward = 1 - 2 * far
    within = z + far * (3 - 2 * z)
    nearest = [3 * far + toward * at for at in (1 - within, 2, 3)]

    def at_z(where):
        return where * 4 + blk % 4, col

    def base(c, p2, p1):
        return ((c * 2 + p2) * 2 + p1) * slab

    def piece(start, where):
        return pl.ds(pl.multiple_of(start + where * size, size), size)

    mine = emb_hbm.at[pl.ds(pl.multiple_of(col * rows, 64), rows)]
    loads = [
        pltpu.make_async_copy(src, dst, local_sem.at[n])
        for n, (src, dst) in enumerate((
            (land_hbm, land_ref), (coef_hbm, coef_ref), (width_hbm, width_ref),
            (lab_hbm, lab_ref), (mine, emb),
        ))
    ]
    for load in loads:
        load.start()

    barrier = pltpu.get_barrier_semaphore()
    peers = [first, second, core] + [at_z(where) for where in nearest]
    for peer in peers:
        pl.semaphore_signal(barrier, inc=1, device_id=peer, device_id_type=pl.DeviceIdType.MESH)

    own = piece(base(col, my2, my1), z)
    for load in loads[:3]:
        load.wait()
    eye = lax.broadcasted_iota(jnp.int32, (size, size), 0) == lax.broadcasted_iota(
        jnp.int32, (size, size), 1
    )
    width_col = jnp.sum(
        jnp.where(eye, width_ref[...].astype(jnp.float32), 0.0), axis=1, keepdims=True
    )
    tail = wide - 128
    split = tail - depth
    lanes = lax.broadcasted_iota(jnp.int32, (size, 128), 1)
    last = jnp.concatenate(
        [
            coef_ref[:, split:].astype(jnp.float32),
            jnp.zeros((size, 128 - (classes - split)), jnp.float32),
        ],
        axis=1,
    )
    last = jnp.where(lanes == classes - split, width_col, last)
    table[own, :depth] = land_ref[...]
    table[own, depth:tail] = coef_ref[:, :split]
    table[own, tail:] = last.astype(jnp.bfloat16)

    pl.semaphore_wait(barrier, len(peers))

    sends = []

    def send(src, dst, recv, device):
        copy = pltpu.make_async_remote_copy(
            src_ref=src, dst_ref=dst, send_sem=send_sem.at[len(sends)], recv_sem=recv,
            device_id=device, device_id_type=pl.DeviceIdType.MESH,
        )
        copy.start()
        sends.append(copy)

    def arrived(dst, recv):
        pltpu.make_async_remote_copy(
            src_ref=dst, dst_ref=dst, send_sem=send_sem.at[0], recv_sem=recv,
            device_id=core, device_id_type=pl.DeviceIdType.MESH,
        ).wait_recv()

    def put(where, recv, device):
        send(table.at[where], table.at[where], recv, device)

    slab_a = base(col, my2, my1)
    slab_b = base(col, my2, 1 - my1)
    slab_c = base(col, 1 - my2, my1)
    slab_d = base(col, 1 - my2, 1 - my1)
    for where in nearest:
        put(own, z_sem.at[z], at_z(where))
    put(own, second_sem.at[0], second)
    put(own, first_sem.at[0], first)
    put(own, core_sem.at[0], core)

    for load in loads[3:]:
        load.wait()
    emb_f = emb[...].astype(jnp.float32)
    eye_rows = lax.broadcasted_iota(jnp.int32, (rows, rows), 0) == lax.broadcasted_iota(
        jnp.int32, (rows, rows), 1
    )
    rows_sq = jnp.sum(jnp.square(emb_f), axis=1, keepdims=True)
    rows_sq = jnp.sum(jnp.where(eye_rows, rows_sq, 0.0), axis=0, keepdims=True)

    around = [z] + nearest

    def from_z_axis(k):
        where = piece(slab_a, around[k])
        arrived(table.at[where], z_sem.at[around[k]])
        put(where, first_sem.at[k], first)
        put(where, second_sem.at[k], second)
        put(where, core_sem.at[k], core)

    def from_first_axis(k):
        where = piece(slab_b, around[k])
        arrived(table.at[where], first_sem.at[k])
        put(where, second_sem.at[4 + k], second)
        put(where, core_sem.at[4 + k], core)

    def from_second_axis(n, k):
        where = piece((slab_c, slab_d)[n], around[k])
        arrived(table.at[where], second_sem.at[4 * n + k])
        put(where, core_sem.at[8 + 4 * n + k], core)

    def widths_of(where):
        end = table[where, tail:].astype(jnp.float32)
        at = lax.broadcasted_iota(jnp.int32, end.shape, 1) == classes - split
        return jnp.sum(jnp.where(at, end, 0.0), axis=1, keepdims=True)

    def forward(start, fresh):
        where = pl.ds(pl.multiple_of(start, half), half)
        land = table[where, :depth]
        cross = lax.dot_general(land, emb[...], NT, preferred_element_type=jnp.float32)
        land_sq = jnp.sum(jnp.square(land.astype(jnp.float32)), axis=1, keepdims=True)
        dist = (rows_sq + land_sq) - 2.0 * cross
        value = jnp.exp(-widths_of(where) * dist).astype(jnp.bfloat16)
        kern[where, :] = value
        part = lax.dot_general(
            value, table[where, depth:], TN, preferred_element_type=jnp.float32
        )
        if fresh:
            logits[...] = part
        else:
            logits[...] += part

    for k in (1, 2, 3):
        from_z_axis(k)
    for k in range(4):
        from_first_axis(k)
    forward(base(col, my2, 0), True)
    for k in range(4):
        from_second_axis(0, k)
    for n, start in enumerate((base(other, my1, my2), base(other, my1, 1 - my2))):
        for k in range(4):
            arrived(table.at[piece(start, around[k])], core_sem.at[4 * n + k])
    forward(base(other, my1, 0), False)
    for k in range(4):
        from_second_axis(1, k)
    forward(base(col, 1 - my2, 0), False)
    for n, start in enumerate((base(other, 1 - my1, my2), base(other, 1 - my1, 1 - my2))):
        for k in range(4):
            arrived(table.at[piece(start, around[k])], core_sem.at[8 + 4 * n + k])
    forward(base(other, 1 - my1, 0), False)

    all_rows = lab_ref.shape[0]
    mine = lax.broadcasted_iota(jnp.int32, (rows, all_rows), 1) == (
        lax.broadcasted_iota(jnp.int32, (rows, all_rows), 0) + col * rows
    )
    label = jnp.sum(
        jnp.where(mine, lab_ref[...].astype(jnp.float32)[None, :], 0.0), axis=1, keepdims=True
    ).astype(jnp.int32)
    place = lax.broadcasted_iota(jnp.int32, logits.shape, 1)
    value = jnp.where(place < classes, logits[...], -jnp.inf)
    expo = jnp.exp(value - jnp.max(value, axis=1, keepdims=True))
    probs = expo / jnp.sum(expo, axis=1, keepdims=True)
    grad[...] = (probs - jnp.where(place == label, 1.0, 0.0)).astype(jnp.bfloat16)

    def terms(start):
        where = pl.ds(pl.multiple_of(start, half), half)
        grad_kernel = lax.dot_general(
            table[where, depth:], grad[...], NT, preferred_element_type=jnp.float32
        )
        tug = (
            2.0 * widths_of(where) * grad_kernel * kern[where, :].astype(jnp.float32)
        ).astype(jnp.bfloat16)
        pull[where, :] = tug
        land = jnp.dot(tug, emb[...], preferred_element_type=jnp.float32)
        land -= jnp.sum(tug.astype(jnp.float32), axis=1, keepdims=True) * table[
            where, :depth
        ].astype(jnp.float32)
        coef = jnp.dot(kern[where, :], grad[...], preferred_element_type=jnp.float32)
        return land, coef

    def part(index):
        return pl.ds(pl.multiple_of(index * slab, slab), slab)

    def for_core(n, p2):
        land, coef = terms(base(other, p2, 0))
        to_core[n, :, :depth] = land.astype(jnp.bfloat16)
        to_core[n, :, depth:] = coef.astype(jnp.bfloat16)
        for m, p1 in enumerate((1 - my2, my2)):
            send(
                to_core.at[n, part(p1)], from_core.at[n, part(p1)],
                back_sem.at[2 * n + m], core,
            )

    def for_self(n, p2):
        land, coef = terms(base(col, p2, 0))
        acc[n, :, :depth] = land
        acc[n, :, depth:] = coef

    def target(p1, where):
        start = p1 * slab + where * size
        return pl.ds(pl.multiple_of(start, size), size)

    order = around[::-1]
    for_core(0, 1 - my1)
    for_self(0, 1 - my2)
    for m, p1 in enumerate((1 - my1, my1)):
        arrived(from_core.at[0, part(p1)], back_sem.at[m])
    for n in range(4):
        for m, p1 in enumerate((1 - my1, my1)):
            where = target(p1, order[n])
            total = acc[0, where, :] + from_core[0, where, :].astype(jnp.float32)
            to_second[n, m] = total.astype(jnp.bfloat16)
            send(to_second.at[n, m], from_second.at[n, m], piece_sem.at[n, m], second)
    for_core(1, my1)
    for_self(1, my2)
    for m, p1 in enumerate((1 - my1, my1)):
        arrived(from_core.at[1, part(p1)], back_sem.at[2 + m])

    def summed(n, m, p1, k):
        where = target(p1, k)
        arrived(from_second.at[n, m], piece_sem.at[n, m])
        return (
            acc[1, where, :]
            + from_core[1, where, :].astype(jnp.float32)
            + from_second[n, m].astype(jnp.float32)
        )

    def pass_first(n):
        to_first[n] = summed(n, 0, 1 - my1, order[n]).astype(jnp.bfloat16)
        send(to_first.at[n], from_first.at[n], piece_sem.at[n, 2], first)

    def collect(n):
        total = summed(n, 1, my1, order[n])
        arrived(from_first.at[n], piece_sem.at[n, 2])
        return total + from_first[n].astype(jnp.float32)

    def pass_z(n):
        to_z[n] = collect(n).astype(jnp.bfloat16)
        send(to_z.at[n], from_z.at[z], back_z_sem.at[z], at_z(order[n]))

    def project(n):
        where = pl.ds(n * slab, slab)
        tug = pull_t[where, :]
        drawn = jnp.dot(tug, table[:, :depth], preferred_element_type=jnp.float32)
        out_emb[where, :] = drawn - jnp.sum(
            tug.astype(jnp.float32), axis=1, keepdims=True
        ) * emb[where, :].astype(jnp.float32)

    pass_first(0)
    pull_t[...] = pull[...].T
    pass_first(1)
    pass_z(0)
    project(0)
    pass_first(2)
    pass_z(1)
    pass_first(3)
    project(1)
    pass_z(2)
    project(2)
    result = collect(3)
    for where in order[:3]:
        arrived(from_z.at[where], back_z_sem.at[where])
        result += from_z[where].astype(jnp.float32)
    out_land[...] = result[:, :depth]
    out_coef[...] = result[:, depth : depth + classes]

    for copy in sends:
        copy.wait_send()


def place_kernel(emb, coef, land, out_emb, out_coef, out_land, sem):
    stores = [
        pltpu.make_async_copy(src, dst, sem.at[n])
        for n, (src, dst) in enumerate(((emb, out_emb), (coef, out_coef), (land, out_land)))
    ]
    for store in stores:
        store.start()
    for store in stores:
        store.wait()


def fused(embeddings, labels, landmarks, coeffs, widths):
    size, depth = landmarks.shape
    classes = coeffs.shape[1]
    rows = embeddings.shape[0] // 2
    padded = (classes // 128 + 1) * 128
    wide = depth + padded
    count, half = 32 * size, 8 * size
    vmem = pl.BlockSpec(memory_space=pltpu.VMEM)
    hbm = pl.BlockSpec(memory_space=pltpu.HBM)
    anywhere = pl.BlockSpec(memory_space=pl.ANY)
    bf16, f32 = jnp.bfloat16, jnp.float32
    out_shape = (
        jax.ShapeDtypeStruct((size, depth), f32),
        jax.ShapeDtypeStruct((size, classes), f32),
        jax.ShapeDtypeStruct((rows, depth), f32),
    )
    results = pl.pallas_call(
        functools.partial(fused_kernel, classes),
        out_shape=tuple(pltpu.VMEM(out.shape, out.dtype) for out in out_shape),
        in_specs=[hbm] * 5,
        out_specs=(vmem,) * 3,
        scratch_shapes=[
            pltpu.VMEM((rows, depth), bf16),
            pltpu.VMEM(labels.shape, labels.dtype),
            pltpu.VMEM(landmarks.shape, bf16),
            pltpu.VMEM(coeffs.shape, bf16),
            pltpu.VMEM((1, size), bf16),
            pltpu.VMEM((count, wide), bf16),
            pltpu.VMEM((count, rows), bf16),
            pltpu.VMEM((count, rows), bf16),
            pltpu.VMEM((rows, count), bf16),
            pltpu.VMEM((rows, padded), f32),
            pltpu.VMEM((rows, padded), bf16),
            pltpu.VMEM((2, half, wide), f32),
            pltpu.VMEM((2, half, wide), bf16),
            pltpu.VMEM((2, half, wide), bf16),
            pltpu.VMEM((4, 2, size, wide), bf16),
            pltpu.VMEM((4, 2, size, wide), bf16),
            pltpu.VMEM((4, size, wide), bf16),
            pltpu.VMEM((4, size, wide), bf16),
            pltpu.VMEM((3, size, wide), bf16),
            pltpu.VMEM((4, size, wide), bf16),
            pltpu.SemaphoreType.DMA((50,)),
            pltpu.SemaphoreType.DMA((4,)),
            pltpu.SemaphoreType.DMA((4,)),
            pltpu.SemaphoreType.DMA((8,)),
            pltpu.SemaphoreType.DMA((16,)),
            pltpu.SemaphoreType.DMA((4,)),
            pltpu.SemaphoreType.DMA((4, 3)),
            pltpu.SemaphoreType.DMA((4,)),
            pltpu.SemaphoreType.DMA((5,)),
        ],
        compiler_params=pltpu.CompilerParams(
            collective_id=0, has_side_effects=True, vmem_limit_bytes=60 * 2**20
        ),
    )(embeddings, labels, landmarks, coeffs, widths[None, :])
    grad_emb, grad_coef, grad_land = pl.pallas_call(
        place_kernel,
        out_shape=out_shape[::-1],
        in_specs=[vmem] * 3,
        out_specs=(anywhere,) * 3,
        scratch_shapes=[pltpu.SemaphoreType.DMA((3,))],
        compiler_params=pltpu.CompilerParams(vmem_limit_bytes=16 * 2**20),
    )(*results[::-1])
    return grad_land, grad_coef, grad_emb


def fits_fused(mesh):
    return mesh.shape["blk"] == 16 and mesh.shape["col"] == 2


def solution(mesh):
    return jax.shard_map(
        fused if fits_fused(mesh) else local,
        mesh=mesh,
        in_specs=(
            P("blk", None),
            P("blk"),
            P(("blk", "col"), None),
            P(("blk", "col"), None),
            P(("blk", "col")),
        ),
        out_specs=(P(("blk", "col"), None), P(("blk", "col"), None), P(("blk", "col"), None)),
        check_vma=False,
    )
```
